32 devices in a mesh: member: 2 (over y), band: 4 (over z), fld: 2 (over x), sub: 2 (over core).
Axes of the slice: x: 2, y: 2, z: 4, core: 2. Of those that a mesh axis runs over, the one named last changes fastest.
Arguments:
- spectra: bfloat16 [8, 16, 3, 2, 1280], P(('member', 'band'), ('fld', 'sub')), parts along dimension 0, may hold values from -2 to 2
- legendre: bfloat16 [4, 1280, 1280], P('band'), may hold values from -0.15625 to 0.15625
- assignment: int32 [4], replicated, may hold values from 0 to 3, each once
- circle_longitudes: int32 [1280], replicated, may hold values from 12 to 5136, as said below
- coriolis: float32 [2, 1280], replicated, may hold values from -1.5 to 1.5
- weights: float32 [2, 1280], replicated, may hold values from 13 to 138
- thickness: float32 [16], P(('fld', 'sub')), may hold values from 0.5 to 5
Outputs:
- tendencies: bfloat16 [8, 16, 3, 2, 1280], P(('member', 'band'), ('fld', 'sub')), parts along dimension 0
The draws below stay inside these ranges and needn't reach their ends.
There are 2 independent parts, one for each index of `member`. The reference program is written for one: setup_inputs(seed, part) draws one part's arguments, and reference() takes and returns one part's arrays. A program takes and returns all parts, laid end to end along the dimension named above; an argument that names none is the same for every part. Nothing has to cross between parts.
Inputs may be any that keep to these rules, and one draw needn't show every extreme that they name: Each value once: slot s holds the wavenumber 320 * assignment[s]. `circle_longitudes`: row h of each hemisphere (h counted from the pole) holds between 12 + 4 h and 20 + 4 h points, a multiple of four, the same in both hemispheres; row 1279 holds 5136.
All inputs are finite; a program needn't handle non-finite values.
Results may differ from the reference program's by a relative error of at most 0.0059.
Values may be sent and summed in bfloat16 or wider, within the bound.
No kernel may reach another device: no remote copies, remote signals or barrier semaphores. Data moves between devices by JAX's collectives and lax.ppermute only.
A program may use at most 128 MiB of HBM per device.

```python
import math
import jax
import jax.numpy as jnp

TRUNCATION = 1279
COEFFS = 1280
LAT_HALF = 1280
WAVES = 4
STRIDE = 320
LEVELS = 16


def draw_circle_longitudes(key, part):
    row_index = jnp.arange(LAT_HALF, dtype=jnp.int32)
    shortfall = jax.random.randint(key, (LAT_HALF,), 0, 3, dtype=jnp.int32)
    shortfall = jnp.where(row_index == LAT_HALF - 1, 0, shortfall)
    return (20 + 4 * row_index - 4 * shortfall).astype(jnp.int32)


def block_levels(key, dims, split, least, largest):
    gain = 1.0
    for position, shards_of in split:
        steps = jax.random.uniform(jax.random.fold_in(jax.random.fold_in(key, 6), position), (shards_of,), jnp.float32, least / len(split), largest / len(split))
        gain = gain * jnp.repeat(jnp.exp(steps), dims[position] // shards_of).reshape((-1,) + (1,) * (len(dims) - 1 - position))
    return gain


def normal_values(key, shape, scale, limit, cuts=(), kind=jnp.bfloat16):
    values = scale * jax.random.normal(key, shape, jnp.float32)
    if cuts:
        values = values * block_levels(key, shape, cuts, -0.22, 0.18)
    return jnp.clip(values, -limit, limit).astype(kind)


def setup_inputs(seed: int = 0, part: int = 0) -> dict:
    splits = jax.random.split(jax.random.key(seed), 8)
    own_keys = jax.random.split(jax.random.fold_in(splits[7], part), 8)
    return {
        "spectra": normal_values(own_keys[0], (WAVES, LEVELS, 3, 2, COEFFS), 0.15, 2.0, ((0, 4), (1, 4))),
        "legendre": normal_values(splits[1], (WAVES, COEFFS, LAT_HALF), COEFFS ** -0.5, 0.15625, ((0, 4),)),
        "assignment": jax.random.permutation(splits[2], WAVES).astype(jnp.int32),
        "circle_longitudes": draw_circle_longitudes(jax.random.fold_in(splits[7], 71), part),
        "coriolis": jnp.clip(jax.random.uniform(splits[4], (2, LAT_HALF), jnp.float32, -1.5, 1.5), -1.5, 1.5),
        "weights": jnp.clip(jnp.exp(jax.random.uniform(splits[5], (2, LAT_HALF), jnp.float32, math.log(13.0), math.log(138.0))), 13.0, 138.0),
        "thickness": jnp.clip(jnp.exp(math.log(5.0) - 2.3025851 * jax.random.uniform(splits[6], (LEVELS,), jnp.float32) ** block_levels(splits[6], (LEVELS,), ((0, 4),), -0.2, 0.2)), 0.5, 5.0),
    }


TWO_PI = 6.283185307179586


def wave_masks(wavenumbers, coeff_count):
    row_index = jnp.arange(coeff_count, dtype=jnp.int32)
    inside = row_index[None, :] < (coeff_count - wavenumbers)[:, None]
    part_index = jnp.arange(2, dtype=jnp.int32)
    real_ok = (part_index[None, :] == 0) | (wavenumbers[:, None] > 0)
    return inside[:, None, :] & real_ok[:, :, None]


def trig_tables(wavenumbers, counts, row_bound):
    positions = jnp.arange(row_bound, dtype=jnp.int32)
    phase_index = (wavenumbers[None, :, None] * positions[None, None, :]) % counts[:, None, None]
    angles = TWO_PI * phase_index.astype(jnp.float32) / counts[:, None, None].astype(jnp.float32)
    inside_row = positions[None, None, :] < counts[:, None, None]
    cosine = jnp.where(inside_row, jnp.cos(angles), 0.0)
    sine_part = jnp.where(inside_row, jnp.sin(angles), 0.0)
    return jnp.stack([cosine, sine_part], axis=1).astype(jnp.bfloat16)


def inverse_factor(wavenumbers, counts):
    resolved = 2 * wavenumbers[None, :] < counts[:, None]
    gain_value = jnp.where(resolved, jnp.where(wavenumbers[None, :] == 0, 1.0, 2.0), 0.0)
    sign_pair = jnp.array([1.0, -1.0], dtype=jnp.float32)
    return gain_value[:, None, :] * sign_pair[None, :, None]


def direct_scale(wavenumbers, counts, quadrature):
    resolved = 2 * wavenumbers[None, :] < counts[:, None]
    unit_multiplier = jnp.where(resolved, 1.0, 0.0) / counts[:, None].astype(jnp.float32)
    sign_pair = jnp.array([1.0, -1.0], dtype=jnp.float32)
    return quadrature[:, :, None, None] * sign_pair[None, None, :, None] * unit_multiplier[:, None, None, :]


def tendency_terms(physical_samples, planetary):
    vorticity = physical_samples[:, :, :, 0]
    spreading_rate_grid = physical_samples[:, :, :, 1]
    thermal_state = physical_samples[:, :, :, 2]
    absolute = vorticity + planetary[:, :, None, None]
    return jnp.stack([-absolute * spreading_rate_grid, absolute * vorticity,
                      0.5 * (vorticity * vorticity + spreading_rate_grid * spreading_rate_grid),
                      -thermal_state * spreading_rate_grid], axis=3).astype(jnp.bfloat16)


def reference(spectra, legendre, assignment, circle_longitudes, coriolis, weights, thickness):
    wavenumbers = (STRIDE * assignment).astype(jnp.int32)
    keeper = wave_masks(wavenumbers, COEFFS)
    masked = jnp.where(keeper[:, None, None, :, :], spectra, jnp.zeros_like(spectra))
    parity = jnp.where(jnp.arange(COEFFS) % 2 == 0, 1.0, -1.0).astype(jnp.float32)
    legendre_wide = legendre.astype(jnp.float32)
    masked_wide = masked.astype(jnp.float32)
    north_part = jnp.einsum('ktp,klfrt->klfrp', legendre_wide, masked_wide)
    austral_portion = jnp.einsum('ktp,klfrt->klfrp', legendre_wide, masked_wide * parity)
    fourier = jnp.stack([north_part, austral_portion], axis=1).astype(jnp.bfloat16)
    group_rows = min(32, LAT_HALF)
    back_parts = []
    for group_offset in range(0, LAT_HALF, group_rows):
        group_end = group_offset + group_rows
        row_bound = 20 + 4 * (group_end - 1)
        row_bound = -(-row_bound // 128) * 128
        counts = circle_longitudes[group_offset:group_end]
        tables = trig_tables(wavenumbers, counts, row_bound)
        gain_lookup = jnp.transpose(inverse_factor(wavenumbers, counts), (2, 1, 0)).astype(jnp.bfloat16)
        coeff_block = fourier[..., group_offset:group_end] * gain_lookup[:, None, None, None, :, :]
        physical_samples = jnp.einsum('kelfrj,jrkx->jelfx', coeff_block.astype(jnp.float32), tables.astype(jnp.float32))
        planetary = jnp.transpose(coriolis[:, group_offset:group_end])
        tendency = tendency_terms(physical_samples, planetary)
        summed = jnp.einsum('jelqx,jrkx->kelqrj', tendency.astype(jnp.float32), tables.astype(jnp.float32))
        quadrature = jnp.transpose(weights[:, group_offset:group_end])
        factor = jnp.transpose(direct_scale(wavenumbers, counts, quadrature), (3, 1, 2, 0))
        back_parts.append((summed * factor[:, :, None, None, :, :]).astype(jnp.bfloat16))
    returned = jnp.concatenate(back_parts, axis=5)
    projected = jnp.einsum('ktp,kelqrp->kelqrt', legendre_wide, returned.astype(jnp.float32))
    combined = projected[:, 0] + parity * projected[:, 1]
    weighted = masked[:, :, 2].astype(jnp.float32) * thickness[None, :, None, None]
    column = jnp.cumsum(weighted[:, ::-1], axis=1)[:, ::-1]
    degree = wavenumbers[:, None] + jnp.arange(COEFFS, dtype=jnp.int32)[None, :]
    laplace = (degree * (degree + 1)).astype(jnp.float32) / float(TRUNCATION * (TRUNCATION + 1))
    divergence_tend = combined[:, :, 1] + laplace[:, None, None, :] * (column + combined[:, :, 2])
    result = jnp.stack([combined[:, :, 0], divergence_tend, combined[:, :, 3]], axis=2)
    result = jnp.where(keeper[:, None, None, :, :], result, 0.0)
    return result.astype(jnp.bfloat16)
```

```python
import functools
import math

import jax
import jax.numpy as jnp
import numpy as np
from jax import lax
from jax.experimental import pallas as pl
from jax.experimental.pallas import tpu as pltpu
from jax.sharding import PartitionSpec as P


FIELDS = 3
TERMS = 4
LANES = 128


def round_up(value, multiple):
    return -(-value // multiple) * multiple


def inverse_kernel(chunk, info_ref, thick_ref, spectra_ref, table_ref, fourier_ref, column_ref, total_ref,
                   rows_scr, table_scr, acc_scr, sems):
    levels, coeffs = spectra_ref.shape[1], spectra_ref.shape[4]
    chunks = coeffs // chunk
    copies = [
        pltpu.make_async_copy(table_ref.at[0, pl.ds(i * chunk, chunk)], table_scr.at[i], sems.at[i])
        for i in range(chunks)
    ]
    for copy in copies:
        copy.start()
    wave = info_ref[0]
    rows = levels * FIELDS * 2
    for level in range(levels):
        for field in range(FIELDS):
            at = (level * FIELDS + field) * 2
            rows_scr[at:at + 2, :] = spectra_ref[0, level, field].astype(jnp.float32)
    coeff = lax.broadcasted_iota(jnp.int32, (rows, coeffs), 1)
    part = lax.broadcasted_iota(jnp.int32, (rows, coeffs), 0) % 2
    keep = (coeff < coeffs - wave) & ((part == 0) | (wave > 0))
    masked = jnp.where(keep, rows_scr[...], 0.0).astype(jnp.bfloat16)
    out_rows = 2 * rows
    place = lax.broadcasted_iota(jnp.int32, (out_rows, rows), 0)
    source = lax.broadcasted_iota(jnp.int32, (out_rows, rows), 1)
    chosen = (place // (2 * levels) == source % (2 * FIELDS)) & (place % levels == source // (2 * FIELDS))
    move = jnp.where(chosen, 1.0, 0.0).astype(jnp.bfloat16)
    spread = jnp.dot(move, masked, preferred_element_type=jnp.float32)
    odd = lax.broadcasted_iota(jnp.int32, (out_rows, coeffs), 1) % 2 == 1
    south = lax.broadcasted_iota(jnp.int32, (out_rows, coeffs), 0) // levels % 2 == 1
    signed = jnp.where(odd & south, -spread, spread).astype(jnp.bfloat16)
    for i in range(chunks):
        copies[i].wait()
        product = jnp.dot(signed[:, i * chunk:(i + 1) * chunk], table_scr[i], preferred_element_type=jnp.float32)
        if i == 0:
            acc_scr[...] = product
        elif i < chunks - 1:
            acc_scr[...] += product
        else:
            fourier_ref[...] = (acc_scr[...] + product).astype(jnp.bfloat16)
    level_at = lax.broadcasted_iota(jnp.int32, (2 * levels, coeffs), 0) % levels
    for r in range(2):
        at = (2 * 2 + r) * 2 * levels
        column = jnp.zeros((2 * levels, coeffs), jnp.float32)
        for level in range(levels):
            weighted = spread[at + level:at + level + 1] * thick_ref[level]
            column += jnp.where(level_at <= level, weighted, 0.0)
        column_ref[r * 2 * levels:(r + 1) * 2 * levels, :] = column
        total_ref[r:r + 1, :] = column[0:1]


def direct_kernel(waves, half, stacked, chunk, info_ref, *refs):
    slots = 1 if stacked else waves
    fourier_refs, refs = refs[:slots], refs[slots:]
    below_refs, refs = refs[:3], refs[3:]
    (synth_ref, analysis_ref, planet_ref, quad_ref, column_ref, table_ref, out_ref,
     table_scr, back_scr, sems) = refs
    levels = out_ref.shape[1]
    coeffs, lats = table_ref.shape[1], table_ref.shape[2]
    pair = 2 * levels
    chunks = coeffs // chunk
    copies = [
        pltpu.make_async_copy(table_ref.at[0, pl.ds(i * chunk, chunk)], table_scr.at[i], sems.at[i])
        for i in range(chunks)
    ]
    for copy in copies:
        copy.start()
    wave = info_ref[0]

    def lat_block(block, carry):
        lanes = pl.ds(pl.multiple_of(block * LANES, LANES), LANES)
        coefs = []
        for k in range(waves):
            fields = []
            for field in range(FIELDS):
                at = field * 2 * pair
                if stacked:
                    both = fourier_refs[0][k, at:at + 2 * pair, lanes]
                else:
                    both = fourier_refs[k][at:at + 2 * pair, lanes]
                both = both.astype(jnp.float32)
                fields.append((both[:pair], both[pair:]))
            coefs.append(fields)
        planet = planet_ref[:, lanes]
        zero = jnp.zeros((pair, LANES), jnp.float32)

        def angle(j, sums):
            even = [zero] * FIELDS
            odd = [zero] * FIELDS
            for k in range(waves):
                harmonic = info_ref[1 + k]
                cosine = synth_ref[harmonic, j, 0:1, lanes]
                sine = synth_ref[harmonic, j, 1:2, lanes]
                for field in range(FIELDS):
                    real, imag = coefs[k][field]
                    even[field] = even[field] + real * cosine
                    odd[field] = odd[field] + imag * sine
            (z_e, d_e, t_e), (z_o, d_o, t_o) = even, odd
            a_e = z_e + planet
            cosine = analysis_ref[j, 0:1, lanes]
            sine = analysis_ref[j, 1:2, lanes]
            kinds = (
                (-(a_e * d_e + z_o * d_o), -(a_e * d_o + z_o * d_e)),
                (a_e * z_e + z_o * z_o, (a_e + z_e) * z_o),
                (0.5 * (z_e * z_e + z_o * z_o + d_e * d_e + d_o * d_o), z_e * z_o + d_e * d_o),
                (-(t_e * d_e + t_o * d_o), -(t_e * d_o + t_o * d_e)),
            )
            out = []
            for q, (in_even, in_odd) in enumerate(kinds):
                out.append(sums[2 * q] + in_even * cosine)
                out.append(sums[2 * q + 1] + in_odd * sine)
            return out

        sums = [zero] * (2 * TERMS)
        if half <= 8:
            for j in range(half):
                sums = angle(j, sums)
        else:
            sums = lax.fori_loop(0, half, angle, sums)
        quad = quad_ref[:, lanes]
        for q in range(TERMS):
            both = jnp.concatenate([sums[2 * q] * quad, sums[2 * q + 1] * quad], axis=0)
            back_scr[q * 2 * pair:(q + 1) * 2 * pair, lanes] = both.astype(jnp.bfloat16)
        return carry

    lax.fori_loop(0, lats // LANES, lat_block, 0)

    back = back_scr[...]
    groups = 2 * FIELDS
    place = lax.broadcasted_iota(jnp.int32, (levels * groups, groups * pair), 0)
    source = lax.broadcasted_iota(jnp.int32, (levels * groups, groups * pair), 1)
    chosen = (place % groups == source // pair) & (place // groups == source % pair)
    move = jnp.where(chosen, 1.0, 0.0).astype(jnp.bfloat16)
    truncation = coeffs - 1
    for i in range(chunks):
        copies[i].wait()
        span = slice(i * chunk, (i + 1) * chunk)
        product = lax.dot_general(back, table_scr[i], (((1,), (1,)), ((), ())), preferred_element_type=jnp.float32)
        coeff = lax.broadcasted_iota(jnp.int32, (pair, chunk), 1) + i * chunk
        lower = lax.broadcasted_iota(jnp.int32, (pair, chunk), 0) < levels
        flip = coeff % 2 == 1
        degree = wave + coeff
        laplace = (degree * (degree + 1)).astype(jnp.float32) / float(truncation * (truncation + 1))
        inside = coeff < coeffs - wave

        def both_rows(q, r):
            at = (2 * q + r) * pair
            rows = product[at:at + pair]
            south = pltpu.roll(rows, levels, 0)
            return rows + jnp.where(flip, -south, south)

        results = []
        for field in range(FIELDS):
            for r in range(2):
                if field == 0:
                    value = both_rows(0, r)
                elif field == 1:
                    column = column_ref[r * pair:(r + 1) * pair, span]
                    for below in below_refs:
                        column = column + below[r:r + 1, span]
                    value = both_rows(1, r) + laplace * (column + both_rows(2, r))
                else:
                    value = both_rows(3, r)
                keep = inside & lower
                if r == 1:
                    keep = keep & (wave > 0)
                results.append(jnp.where(keep, value, 0.0))
        stacked_rows = jnp.concatenate(results, axis=0).astype(jnp.bfloat16)
        ordered = jnp.dot(move, stacked_rows, preferred_element_type=jnp.float32)
        for level in range(levels):
            for field in range(FIELDS):
                at = (level * FIELDS + field) * 2
                out_ref[0, level, field, :, span] = ordered[at:at + 2].astype(jnp.bfloat16)


def angle_tables(waves, spacing, counts, harmonic):
    most = 3 * (waves - 1) + 1
    half = most // 2 + 1
    tries = jnp.arange(1, most, dtype=jnp.int32)[:, None]
    fits = spacing * tries % counts[None, :] == 0
    angles = jnp.min(jnp.where(fits, tries, most), axis=0)
    which = (jnp.arange(1, most + 1, dtype=jnp.int32)[:, None] == angles[None, :]).astype(jnp.float32)
    n = np.arange(1, most + 1)[None, None, :]
    a = np.arange(waves)[:, None, None]
    j = np.arange(half)[None, :, None]
    turn = 2.0 * np.pi * (a * j % n) / n
    live = 2 * j <= n
    alone = (j == 0) | (2 * j == n)
    basis = np.stack([np.cos(turn), -np.sin(turn)], axis=2)
    share = np.where(live, np.where(alone, 1.0, 2.0), 0.0) / n
    table = np.concatenate([basis.reshape(-1, most), np.broadcast_to(share, (1, half, most)).reshape(-1, most)])
    looked = jnp.dot(jnp.asarray(table, jnp.float32), which, precision=lax.Precision.HIGHEST)
    trig = looked[:waves * half * 2].reshape(waves, half, 2, -1)
    share = looked[waves * half * 2:]
    order = jnp.arange(waves, dtype=jnp.int32)
    seen = 2 * spacing * order[:, None] < counts[None, :]
    gain = jnp.where(seen, jnp.where(order[:, None] == 0, 1.0, 2.0), 0.0)
    synthesis = trig * gain[:, None, None, :]
    own = lax.dynamic_index_in_dim(trig, harmonic, 0, False)
    own_seen = 2 * spacing * harmonic < counts
    analysis = own * jnp.where(own_seen, share, 0.0)[:, None, :]
    return half, synthesis, analysis


def on_device(spectra, legendre, assignment, circle_longitudes, coriolis, weights, thickness):
    levels, coeffs = spectra.shape[1], spectra.shape[4]
    lats = legendre.shape[2]
    waves = lax.axis_size("band")
    me = lax.axis_index("band")
    spacing = coeffs // waves
    few = waves <= 8
    if few:
        order = (me - jnp.arange(waves, dtype=jnp.int32)) % waves
    else:
        order = jnp.arange(waves, dtype=jnp.int32)
    own_harmonic = lax.dynamic_index_in_dim(assignment, me, 0, False)
    info = jnp.concatenate([(spacing * own_harmonic)[None], assignment[order]])
    pair = 2 * levels
    rows = levels * FIELDS * 2
    chunk = 256 if coeffs % 256 == 0 else LANES
    chunks = coeffs // chunk
    smem = pl.BlockSpec(memory_space=pltpu.SMEM)
    vmem = pl.BlockSpec(memory_space=pltpu.VMEM)
    hbm = pl.BlockSpec(memory_space=pl.ANY)

    fourier, column, total = pl.pallas_call(
        functools.partial(inverse_kernel, chunk),
        out_shape=(
            jax.ShapeDtypeStruct((2 * rows, lats), jnp.bfloat16),
            jax.ShapeDtypeStruct((2 * pair, coeffs), jnp.float32),
            jax.ShapeDtypeStruct((2, coeffs), jnp.float32),
        ),
        in_specs=[smem, smem, vmem, hbm],
        out_specs=(vmem, vmem, vmem),
        scratch_shapes=[
            pltpu.VMEM((rows, coeffs), jnp.float32),
            pltpu.VMEM((chunks, chunk, lats), jnp.bfloat16),
            pltpu.VMEM((2 * rows, lats), jnp.float32),
            pltpu.SemaphoreType.DMA((chunks,)),
        ],
        compiler_params=pltpu.CompilerParams(vmem_limit_bytes=24 << 20),
        name="inverse",
    )(info, thickness, spectra, legendre)

    deep = ("fld", "sub")
    places = lax.axis_size(deep)
    belows = [
        lax.ppermute(total, deep, [(i, i - k) for i in range(k, places)]) for k in range(1, places)
    ]
    if len(belows) > 3:
        belows = [belows[0], belows[1], functools.reduce(jnp.add, belows[2:])]
    while len(belows) < 3:
        belows.append(jnp.zeros_like(total))
    if few:
        fouriers = [fourier] + [
            lax.ppermute(fourier, "band", [(i, (i + k) % waves) for i in range(waves)]) for k in range(1, waves)
        ]
    else:
        fouriers = [lax.all_gather(fourier, "band")]
    half, synthesis, analysis = angle_tables(waves, spacing, circle_longitudes, own_harmonic)
    planet = jnp.repeat(coriolis, levels, axis=0)
    quad = jnp.repeat(weights, levels, axis=0)

    (tendencies,) = pl.pallas_call(
        functools.partial(direct_kernel, waves, half, not few, chunk),
        out_shape=(jax.ShapeDtypeStruct(spectra.shape, jnp.bfloat16),),
        in_specs=[smem] + [vmem] * (len(fouriers) + 3 + 5) + [hbm],
        out_specs=(vmem,),
        scratch_shapes=[
            pltpu.VMEM((chunks, chunk, lats), jnp.bfloat16),
            pltpu.VMEM((TERMS * 2 * pair, lats), jnp.bfloat16),
            pltpu.SemaphoreType.DMA((chunks,)),
        ],
        compiler_params=pltpu.CompilerParams(vmem_limit_bytes=(24 if few else 56) << 20),
        name="direct",
    )(info, *fouriers, *belows, synthesis, analysis, planet, quad, column, legendre)
    return tendencies


def solution(mesh):
    in_specs = (
        P(("member", "band"), ("fld", "sub"), None, None, None),
        P("band", None, None),
        P(),
        P(),
        P(),
        P(),
        P(("fld", "sub")),
    )
    out_specs = P(("member", "band"), ("fld", "sub"), None, None, None)
    return jax.shard_map(
        on_device, mesh=mesh, in_specs=in_specs, out_specs=out_specs, check_vma=False
    )
```

```python
import functools
import math

import jax
import jax.numpy as jnp
from jax import lax
from jax.experimental import pallas as pl
from jax.experimental.pallas import tpu as pltpu
from jax.sharding import PartitionSpec as P


FIELDS = 3
TERMS = 4
LANES = 128
SUBLANES = 8


def round_up(value, multiple):
    return -(-value // multiple) * multiple


def slot_order(waves, few, slot):
    if not few:
        return slot
    return lax.rem(lax.axis_index("band") + waves - slot, waves)


def inverse_kernel(spacing, chunk, assign_ref, spectra_ref, table_ref, fourier_ref,
                   spectra_scr, rows_scr, table_scr, acc_scr, sem, sems):
    levels, coeffs = spectra_ref.shape[1], spectra_ref.shape[4]
    chunks = coeffs // chunk
    first = pltpu.make_async_copy(spectra_ref, spectra_scr, sem)
    first.start()
    copies = [
        pltpu.make_async_copy(table_ref.at[0, pl.ds(i * chunk, chunk)], table_scr.at[i], sems.at[i])
        for i in range(chunks)
    ]
    for copy in copies:
        copy.start()
    wave = spacing * assign_ref[lax.axis_index("band")]
    rows = levels * FIELDS * 2
    first.wait()
    for level in range(levels):
        for field in range(FIELDS):
            at = (level * FIELDS + field) * 2
            rows_scr[at:at + 2, :] = spectra_scr[0, level, field].astype(jnp.float32)
    coeff = lax.broadcasted_iota(jnp.int32, (rows, coeffs), 1)
    part = lax.broadcasted_iota(jnp.int32, (rows, coeffs), 0) % 2
    keep = (coeff < coeffs - wave) & ((part == 0) | (wave > 0))
    masked = jnp.where(keep, rows_scr[...], 0.0).astype(jnp.bfloat16)
    out_rows = 2 * rows
    place = lax.broadcasted_iota(jnp.int32, (out_rows, rows), 0)
    source = lax.broadcasted_iota(jnp.int32, (out_rows, rows), 1)
    chosen = (place // (2 * levels) == source % (2 * FIELDS)) & (place % levels == source // (2 * FIELDS))
    move = jnp.where(chosen, 1.0, 0.0).astype(jnp.bfloat16)
    spread = jnp.dot(move, masked, preferred_element_type=jnp.float32)
    odd = lax.broadcasted_iota(jnp.int32, (out_rows, coeffs), 1) % 2 == 1
    south = lax.broadcasted_iota(jnp.int32, (out_rows, coeffs), 0) // levels % 2 == 1
    signed = jnp.where(odd & south, -spread, spread).astype(jnp.bfloat16)
    for i in range(chunks):
        copies[i].wait()
        product = jnp.dot(signed[:, i * chunk:(i + 1) * chunk], table_scr[i], preferred_element_type=jnp.float32)
        if i == 0:
            acc_scr[...] = product
        elif i < chunks - 1:
            acc_scr[...] += product
        else:
            fourier_ref[...] = (acc_scr[...] + product).astype(jnp.bfloat16)


def cos_sin(turns):
    angle = turns * (2.0 * math.pi)
    square = angle * angle
    cosine = jnp.full_like(angle, 1.0 / math.factorial(18) * -1.0)
    sine = jnp.full_like(angle, 1.0 / math.factorial(17))
    for n in range(8, -1, -1):
        cosine = cosine * square + (-1.0) ** n / math.factorial(2 * n)
        if n < 8:
            sine = sine * square + (-1.0) ** n / math.factorial(2 * n + 1)
    return cosine, sine * angle


def aux_layout(waves, levels):
    half = (3 * (waves - 1) + 1) // 2 + 1
    angles = round_up(half, SUBLANES)
    pair = 2 * levels
    sizes = (("cosine", waves * angles), ("sine", waves * angles), ("own_cosine", angles), ("own_sine", angles),
             ("planet", pair), ("quad", pair), ("column", 2 * pair))
    starts, at = {}, 0
    for name, size in sizes:
        starts[name] = at
        at += size
    return half, angles, starts, at


def aux_kernel(waves, few, spacing, assign_ref, thick_ref, counts_ref, planet_ref, quad_ref, spectra_ref, after_ref,
               aux_ref, total_ref):
    del after_ref
    levels, coeffs = spectra_ref.shape[1], spectra_ref.shape[4]
    pair = 2 * levels
    half, angles, starts, _ = aux_layout(waves, levels)
    lats = aux_ref.shape[1]
    counts = counts_ref[...].astype(jnp.float32)
    most = 3 * (waves - 1) + 1

    def attempt(p, least):
        points = p * float(spacing)
        left = points - counts * jnp.floor((points + 0.5) / counts)
        return jnp.where((left == 0.0) & (least > p), p, least)

    least = jnp.full((1, lats), float(most), jnp.float32)
    if most <= 16:
        for p in range(1, most):
            least = attempt(float(p), least)
    else:
        least = lax.fori_loop(1, most, lambda p, least: attempt(p.astype(jnp.float32), least), least)
    number = jnp.broadcast_to(least, (angles, lats))
    j = lax.broadcasted_iota(jnp.int32, (angles, lats), 0).astype(jnp.float32)
    share = jnp.where(2.0 * j <= number, jnp.where((j == 0.0) | (2.0 * j == number), 1.0, 2.0), 0.0) / number

    def slot(k, carry):
        harmonic = assign_ref[slot_order(waves, few, k)]
        turn = j * harmonic.astype(jnp.float32)
        turn = turn - number * jnp.floor((turn + 0.5) / number)
        turn = jnp.where(2.0 * turn > number, turn - number, turn) / number
        cosine, sine = cos_sin(turn)
        seen = (2 * spacing * harmonic).astype(jnp.float32) < counts
        gain = jnp.where(seen, jnp.where(harmonic == 0, 1.0, 2.0), 0.0)
        at = pl.ds(pl.multiple_of(starts["cosine"] + k * angles, SUBLANES), angles)
        aux_ref[at, :] = cosine * gain
        at = pl.ds(pl.multiple_of(starts["sine"] + k * angles, SUBLANES), angles)
        aux_ref[at, :] = -sine * gain
        mine = share * jnp.where(seen, 1.0, 0.0)
        own = k == (0 if few else lax.axis_index("band"))

        @pl.when(own)
        def _():
            aux_ref[starts["own_cosine"]:starts["own_cosine"] + angles, :] = cosine * mine
            aux_ref[starts["own_sine"]:starts["own_sine"] + angles, :] = -sine * mine

        return carry

    lax.fori_loop(0, waves, slot, 0)
    north = lax.broadcasted_iota(jnp.int32, (pair, lats), 0) < levels
    for name, ref in (("planet", planet_ref), ("quad", quad_ref)):
        aux_ref[starts[name]:starts[name] + pair, :] = jnp.where(north, ref[0:1, :], ref[1:2, :])
    wave = spacing * assign_ref[lax.axis_index("band")]
    level_at = lax.broadcasted_iota(jnp.int32, (pair, coeffs), 0) % levels
    inside = lax.broadcasted_iota(jnp.int32, (2, coeffs), 1) < coeffs - wave
    keep = inside & ((lax.broadcasted_iota(jnp.int32, (2, coeffs), 0) == 0) | (wave > 0))
    columns = [jnp.zeros((pair, coeffs), jnp.float32)] * 2
    for level in range(levels):
        weighted = jnp.where(keep, spectra_ref[0, level, 2].astype(jnp.float32), 0.0) * thick_ref[level]
        for r in range(2):
            columns[r] += jnp.where(level_at <= level, weighted[r:r + 1], 0.0)
    for r in range(2):
        at = starts["column"] + r * pair
        aux_ref[at:at + pair, :] = columns[r]
        total_ref[r:r + 1, :] = columns[r][0:1]


def direct_kernel(waves, few, spacing, belows, chunk, assign_ref, *refs):
    slots = waves if few else 1
    fourier_refs, refs = refs[:slots], refs[slots:]
    below_refs, refs = refs[:belows], refs[belows:]
    aux_ref, table_ref, out_ref, fourier_scr, back_scr, sems = refs
    levels = out_ref.shape[1]
    coeffs, lats = table_ref.shape[1], table_ref.shape[2]
    half, angles, starts, _ = aux_layout(waves, levels)
    pair = 2 * levels
    chunks = coeffs // chunk
    copies = []
    for k, ref in enumerate(fourier_refs):
        target = fourier_scr.at[k] if few else fourier_scr
        copies.append(pltpu.make_async_copy(ref, target, sems.at[k]))
        copies[-1].start()
    wave = spacing * assign_ref[lax.axis_index("band")]
    for copy in copies:
        copy.wait()

    def lat_block(block, carry):
        lanes = pl.ds(pl.multiple_of(block * LANES, LANES), LANES)
        coefs = []
        for k in range(waves):
            fields = []
            for field in range(FIELDS):
                at = field * 2 * pair
                both = fourier_scr[k, at:at + 2 * pair, lanes].astype(jnp.float32)
                fields.append((both[:pair], both[pair:]))
            coefs.append(fields)
        planet = aux_ref[starts["planet"]:starts["planet"] + pair, lanes]
        zero = jnp.zeros((pair, LANES), jnp.float32)

        def trig(name, k, j):
            group, row = j
            at = starts[name] + k * angles + group * SUBLANES
            if isinstance(group, int):
                return aux_ref[at + row:at + row + 1, lanes]
            return aux_ref[pl.ds(pl.multiple_of(at, SUBLANES), SUBLANES), lanes][row:row + 1]

        def angle(j, sums):
            even = [zero] * FIELDS
            odd = [zero] * FIELDS
            for k in range(waves):
                cosine = trig("cosine", k, j)
                sine = trig("sine", k, j)
                for field in range(FIELDS):
                    real, imag = coefs[k][field]
                    even[field] = even[field] + real * cosine
                    odd[field] = odd[field] + imag * sine
            (z_e, d_e, t_e), (z_o, d_o, t_o) = even, odd
            a_e = z_e + planet
            cosine = trig("own_cosine", 0, j)
            sine = trig("own_sine", 0, j)
            kinds = (
                (-(a_e * d_e + z_o * d_o), -(a_e * d_o + z_o * d_e)),
                (a_e * z_e + z_o * z_o, (a_e + z_e) * z_o),
                (0.5 * (z_e * z_e + z_o * z_o + d_e * d_e + d_o * d_o), z_e * z_o + d_e * d_o),
                (-(t_e * d_e + t_o * d_o), -(t_e * d_o + t_o * d_e)),
            )
            out = []
            for q, (in_even, in_odd) in enumerate(kinds):
                out.append(sums[2 * q] + in_even * cosine)
                out.append(sums[2 * q + 1] + in_odd * sine)
            return out

        sums = [zero] * (2 * TERMS)
        if half <= SUBLANES:
            for row in range(half):
                sums = angle((0, row), sums)
        else:
            def group(g, sums):
                for row in range(SUBLANES):
                    sums = angle((g, row), sums)
                return sums

            sums = lax.fori_loop(0, angles // SUBLANES, group, sums)
        quad = aux_ref[starts["quad"]:starts["quad"] + pair, lanes]
        for q in range(TERMS):
            both = jnp.concatenate([sums[2 * q] * quad, sums[2 * q + 1] * quad], axis=0)
            back_scr[q * 2 * pair:(q + 1) * 2 * pair, lanes] = both.astype(jnp.bfloat16)
        return carry

    lax.fori_loop(0, lats // LANES, lat_block, 0)

    back = back_scr[...]
    groups = 2 * FIELDS
    place = lax.broadcasted_iota(jnp.int32, (levels * groups, groups * pair), 0)
    source = lax.broadcasted_iota(jnp.int32, (levels * groups, groups * pair), 1)
    chosen = (place % groups == source // pair) & (place // groups == source % pair)
    move = jnp.where(chosen, 1.0, 0.0).astype(jnp.bfloat16)
    truncation = coeffs - 1
    for i in range(chunks):
        span = slice(i * chunk, (i + 1) * chunk)
        product = lax.dot_general(back, table_ref[0, span, :], (((1,), (1,)), ((), ())),
                                  preferred_element_type=jnp.float32)
        coeff = lax.broadcasted_iota(jnp.int32, (pair, chunk), 1) + i * chunk
        lower = lax.broadcasted_iota(jnp.int32, (pair, chunk), 0) < levels
        flip = coeff % 2 == 1
        degree = wave + coeff
        laplace = (degree * (degree + 1)).astype(jnp.float32) / float(truncation * (truncation + 1))
        inside = coeff < coeffs - wave

        def both_rows(q, r):
            at = (2 * q + r) * pair
            rows = product[at:at + pair]
            south = pltpu.roll(rows, levels, 0)
            return rows + jnp.where(flip, -south, south)

        results = []
        for field in range(FIELDS):
            for r in range(2):
                if field == 0:
                    value = both_rows(0, r)
                elif field == 1:
                    at = starts["column"] + r * pair
                    column = aux_ref[at:at + pair, span]
                    for below in below_refs:
                        column = column + below[r:r + 1, span]
                    value = both_rows(1, r) + laplace * (column + both_rows(2, r))
                else:
                    value = both_rows(3, r)
                keep = inside & lower
                if r == 1:
                    keep = keep & (wave > 0)
                results.append(jnp.where(keep, value, 0.0))
        stacked_rows = jnp.concatenate(results, axis=0).astype(jnp.bfloat16)
        ordered = jnp.dot(move, stacked_rows, preferred_element_type=jnp.float32)
        for level in range(levels):
            for field in range(FIELDS):
                at = (level * FIELDS + field) * 2
                out_ref[0, level, field, :, span] = ordered[at:at + 2].astype(jnp.bfloat16)


def on_device(spectra, legendre, assignment, circle_longitudes, coriolis, weights, thickness):
    levels, coeffs = spectra.shape[1], spectra.shape[4]
    lats = legendre.shape[2]
    waves = lax.axis_size("band")
    spacing = coeffs // waves
    few = waves <= 8
    pair = 2 * levels
    rows = levels * FIELDS * 2
    chunk = 256 if coeffs % 256 == 0 else LANES
    chunks = coeffs // chunk
    smem = pl.BlockSpec(memory_space=pltpu.SMEM)
    vmem = pl.BlockSpec(memory_space=pltpu.VMEM)
    hbm = pl.BlockSpec(memory_space=pltpu.HBM)
    anywhere = pl.BlockSpec(memory_space=pl.ANY)

    fourier = pl.pallas_call(
        functools.partial(inverse_kernel, spacing, chunk),
        out_shape=jax.ShapeDtypeStruct((2 * rows, lats), jnp.bfloat16),
        in_specs=[smem, hbm, hbm],
        out_specs=vmem,
        scratch_shapes=[
            pltpu.VMEM(spectra.shape, jnp.bfloat16),
            pltpu.VMEM((rows, coeffs), jnp.float32),
            pltpu.VMEM((chunks, chunk, lats), jnp.bfloat16),
            pltpu.VMEM((2 * rows, lats), jnp.float32),
            pltpu.SemaphoreType.DMA,
            pltpu.SemaphoreType.DMA((chunks,)),
        ],
        compiler_params=pltpu.CompilerParams(vmem_limit_bytes=24 << 20),
        name="inverse",
    )(assignment, spectra, legendre)

    if few:
        fouriers = [fourier] + [
            lax.ppermute(fourier, "band", [(i, (i + k) % waves) for i in range(waves)]) for k in range(1, waves)
        ]
    else:
        fouriers = [lax.all_gather(fourier, "band")]

    half, angles, starts, aux_rows = aux_layout(waves, levels)
    aux, total = pl.pallas_call(
        functools.partial(aux_kernel, waves, few, spacing),
        out_shape=(
            jax.ShapeDtypeStruct((aux_rows, lats), jnp.float32),
            jax.ShapeDtypeStruct((2, coeffs), jnp.float32),
        ),
        in_specs=[smem, smem, vmem, vmem, vmem, vmem, anywhere],
        out_specs=(vmem, vmem),
        compiler_params=pltpu.CompilerParams(vmem_limit_bytes=(16 if few else 48) << 20),
        name="tables",
    )(assignment, thickness, circle_longitudes.reshape(1, lats), coriolis, weights, spectra, fourier)

    deep = ("fld", "sub")
    places = lax.axis_size(deep)
    belows = [
        lax.ppermute(total, deep, [(i, i - k) for i in range(k, places)]) for k in range(1, places)
    ]

    return pl.pallas_call(
        functools.partial(direct_kernel, waves, few, spacing, len(belows), chunk),
        out_shape=jax.ShapeDtypeStruct(spectra.shape, jnp.bfloat16),
        in_specs=[smem] + [anywhere] * len(fouriers) + [vmem] * (len(belows) + 2),
        out_specs=vmem,
        scratch_shapes=[
            pltpu.VMEM((waves, 2 * rows, lats), jnp.bfloat16),
            pltpu.VMEM((TERMS * 2 * pair, lats), jnp.bfloat16),
            pltpu.SemaphoreType.DMA((len(fouriers),)),
        ],
        compiler_params=pltpu.CompilerParams(vmem_limit_bytes=(24 if few else 56) << 20),
        name="direct",
    )(assignment, *fouriers, *belows, aux, legendre)


def solution(mesh):
    in_specs = (
        P(("member", "band"), ("fld", "sub"), None, None, None),
        P("band", None, None),
        P(),
        P(),
        P(),
        P(),
        P(("fld", "sub")),
    )
    out_specs = P(("member", "band"), ("fld", "sub"), None, None, None)
    return jax.shard_map(
        on_device, mesh=mesh, in_specs=in_specs, out_specs=out_specs, check_vma=False
    )
```

```python
import functools
import math

import jax
import jax.numpy as jnp
from jax import lax
from jax.experimental import pallas as pl
from jax.experimental.pallas import tpu as pltpu
from jax.sharding import PartitionSpec as P


FIELDS = 3
TERMS = 4
LANES = 128
SUBLANES = 8


def round_up(value, multiple):
    return -(-value // multiple) * multiple


def slot_position(waves, few, slot):
    return lax.axis_index("band") ^ slot if few else slot


def spectra_kernel(spacing, assign_ref, thick_ref, spectra_ref, signed_ref, total_ref,
                   assign_scr, thick_scr, spectra_scr, rows_scr, sems):
    copies = [
        pltpu.make_async_copy(source, target, sems.at[i])
        for i, (source, target) in enumerate(
            ((assign_ref, assign_scr), (thick_ref, thick_scr), (spectra_ref, spectra_scr)))
    ]
    for copy in copies:
        copy.start()
    levels, coeffs = spectra_ref.shape[1], spectra_ref.shape[4]
    rows = levels * FIELDS * 2
    out_rows = 2 * rows
    place = lax.broadcasted_iota(jnp.int32, (out_rows, rows), 0)
    source = lax.broadcasted_iota(jnp.int32, (out_rows, rows), 1)
    chosen = (place // (2 * levels) == source % (2 * FIELDS)) & (place % levels == source // (2 * FIELDS))
    move = jnp.where(chosen, 1.0, 0.0).astype(jnp.bfloat16)
    for copy in copies:
        copy.wait()
    wave = spacing * assign_scr[lax.axis_index("band")]
    for level in range(levels):
        for field in range(FIELDS):
            at = (level * FIELDS + field) * 2
            rows_scr[at:at + 2, :] = spectra_scr[0, level, field].astype(jnp.float32)
    coeff = lax.broadcasted_iota(jnp.int32, (rows, coeffs), 1)
    part = lax.broadcasted_iota(jnp.int32, (rows, coeffs), 0) % 2
    keep = (coeff < coeffs - wave) & ((part == 0) | (wave > 0))
    masked = jnp.where(keep, rows_scr[...], 0.0).astype(jnp.bfloat16)
    spread = jnp.dot(move, masked, preferred_element_type=jnp.float32)
    odd = lax.broadcasted_iota(jnp.int32, (out_rows, coeffs), 1) % 2 == 1
    south = lax.broadcasted_iota(jnp.int32, (out_rows, coeffs), 0) // levels % 2 == 1
    signed_ref[...] = jnp.where(odd & south, -spread, spread).astype(jnp.bfloat16)
    for r in range(2):
        at = (2 * 2 + r) * 2 * levels
        total = spread[at:at + 1] * thick_scr[0]
        for level in range(1, levels):
            total += spread[at + level:at + level + 1] * thick_scr[level]
        total_ref[r:r + 1, :] = total


def cos_sin(turns):
    angle = turns * (2.0 * math.pi)
    square = angle * angle
    cosine = jnp.full_like(angle, -1.0 / math.factorial(18))
    sine = jnp.full_like(angle, 1.0 / math.factorial(17))
    for n in range(8, -1, -1):
        cosine = cosine * square + (-1.0) ** n / math.factorial(2 * n)
        if n < 8:
            sine = sine * square + (-1.0) ** n / math.factorial(2 * n + 1)
    return cosine, sine * angle


def aux_layout(waves, levels):
    half = (3 * (waves - 1) + 1) // 2 + 1
    angles = round_up(half, SUBLANES)
    pair = 2 * levels
    sizes = (("cosine", waves * angles), ("sine", waves * angles), ("own_cosine", angles), ("own_sine", angles),
             ("planet", pair), ("quad", pair), ("column", 2 * pair), ("keep", 2), ("laplace", 1))
    starts, at = {}, 0
    for name, size in sizes:
        starts[name] = at
        at += size
    return half, angles, starts, round_up(at, SUBLANES)


def aux_kernel(waves, few, spacing, assign_ref, thick_ref, counts_ref, planet_ref, quad_ref, spectra_ref, after_ref,
               aux_ref):
    del after_ref
    levels, coeffs = spectra_ref.shape[1], spectra_ref.shape[4]
    pair = 2 * levels
    half, angles, starts, _ = aux_layout(waves, levels)
    lats = aux_ref.shape[1]
    counts = counts_ref[...].astype(jnp.float32)
    most = 3 * (waves - 1) + 1

    def attempt(p, least):
        points = p * float(spacing)
        left = points - counts * jnp.floor((points + 0.5) / counts)
        return jnp.where((left == 0.0) & (least > p), p, least)

    least = jnp.full((1, lats), float(most), jnp.float32)
    if most <= 16:
        for p in range(1, most):
            least = attempt(float(p), least)
    else:
        least = lax.fori_loop(1, most, lambda p, least: attempt(p.astype(jnp.float32), least), least)
    number = jnp.broadcast_to(least, (angles, lats))
    j = lax.broadcasted_iota(jnp.int32, (angles, lats), 0).astype(jnp.float32)
    share = jnp.where(2.0 * j <= number, jnp.where((j == 0.0) | (2.0 * j == number), 1.0, 2.0), 0.0) / number

    def slot(k, carry):
        harmonic = assign_ref[slot_position(waves, few, k)]
        turn = j * harmonic.astype(jnp.float32)
        turn = turn - number * jnp.floor((turn + 0.5) / number)
        turn = jnp.where(2.0 * turn > number, turn - number, turn) / number
        cosine, sine = cos_sin(turn)
        seen = (2 * spacing * harmonic).astype(jnp.float32) < counts
        gain = jnp.where(seen, jnp.where(harmonic == 0, 1.0, 2.0), 0.0)
        at = pl.ds(pl.multiple_of(starts["cosine"] + k * angles, SUBLANES), angles)
        aux_ref[at, :] = cosine * gain
        at = pl.ds(pl.multiple_of(starts["sine"] + k * angles, SUBLANES), angles)
        aux_ref[at, :] = -sine * gain
        mine = share * jnp.where(seen, 1.0, 0.0)
        own = k == (0 if few else lax.axis_index("band"))

        @pl.when(own)
        def _():
            aux_ref[starts["own_cosine"]:starts["own_cosine"] + angles, :] = cosine * mine
            aux_ref[starts["own_sine"]:starts["own_sine"] + angles, :] = -sine * mine

        return carry

    lax.fori_loop(0, waves, slot, 0)
    north = lax.broadcasted_iota(jnp.int32, (pair, lats), 0) < levels
    for name, ref in (("planet", planet_ref), ("quad", quad_ref)):
        aux_ref[starts[name]:starts[name] + pair, :] = jnp.where(north, ref[0:1, :], ref[1:2, :])
    wave = spacing * assign_ref[lax.axis_index("band")]
    level_at = lax.broadcasted_iota(jnp.int32, (pair, coeffs), 0) % levels
    coeff = lax.broadcasted_iota(jnp.int32, (2, coeffs), 1)
    keep = (coeff < coeffs - wave) & ((lax.broadcasted_iota(jnp.int32, (2, coeffs), 0) == 0) | (wave > 0))
    columns = [jnp.zeros((pair, coeffs), jnp.float32)] * 2
    for level in range(levels):
        weighted = jnp.where(keep, spectra_ref[0, level, 2].astype(jnp.float32), 0.0) * thick_ref[level]
        for r in range(2):
            columns[r] += jnp.where(level_at <= level, weighted[r:r + 1], 0.0)
    for r in range(2):
        at = starts["column"] + r * pair
        aux_ref[at:at + pair, :] = columns[r]
    aux_ref[starts["keep"]:starts["keep"] + 2, :] = jnp.where(keep, 1.0, 0.0)
    degree = wave + coeff[0:1]
    truncation = coeffs - 1
    aux_ref[starts["laplace"]:starts["laplace"] + 1, :] = (
        (degree * (degree + 1)).astype(jnp.float32) / float(truncation * (truncation + 1)))


def arrival(slots):
    return (2, 0, 1) if slots == 3 else range(slots)


def direct_kernel(waves, few, belows, begin, trim, parts, last, *refs):
    own_ref, refs = refs[0], refs[1:]
    slot_refs = [None] * len(parts)
    for at in arrival(len(parts)):
        slot_refs[at] = refs[:parts[at]]
        refs = refs[parts[at]:]
    below_refs, refs = refs[:belows], refs[belows:]
    aux_ref, table_ref, refs = refs[0], refs[1], refs[2:]
    if begin > 0:
        earlier_ref, refs = refs[0], refs[1:]
    if last:
        out_ref, back_scr, out_scr, below_scr, sems = refs
        place = lax.axis_index(("fld", "sub"))
        (below_ref,) = below_refs
        below = jnp.zeros(below_ref.shape[1:], jnp.float32)
        for p in range(1, below_ref.shape[0]):
            below += jnp.where(place < p, below_ref[p], 0.0)
        below_scr[...] = below
        levels = out_scr.shape[1]
    else:
        partial_ref, back_scr = refs
        levels = back_scr.shape[0] // (4 * TERMS)
    chunks, lats, chunk = table_ref.shape
    half, angles, starts, _ = aux_layout(waves, levels)
    pair = 2 * levels
    zero = jnp.zeros((pair, LANES), jnp.float32)

    def products(lane, slots):
        here = pl.ds(lane, LANES)
        lanes = pl.ds(begin + lane, LANES)
        coefs = []
        for k in range(slots):
            fields = []
            for field in range(FIELDS):
                rows = slice(field * 2 * pair, (field + 1) * 2 * pair)
                if not few:
                    both = slot_refs[0][0][k, rows, here].astype(jnp.float32)
                elif k == 0:
                    both = own_ref[rows, here].astype(jnp.float32)
                else:
                    there = pl.ds(lane - trim, LANES)
                    both = slot_refs[k - 1][0][rows, there].astype(jnp.float32)
                    for ref in slot_refs[k - 1][1:]:
                        both = both + ref[rows, there].astype(jnp.float32)
                fields.append((both[:pair], both[pair:]))
            coefs.append(fields)
        planet = aux_ref[starts["planet"]:starts["planet"] + pair, lanes]

        def trig(name, k, j):
            group, row = j
            at = starts[name] + k * angles + group * SUBLANES
            if isinstance(group, int):
                return aux_ref[at + row:at + row + 1, lanes]
            return aux_ref[pl.ds(pl.multiple_of(at, SUBLANES), SUBLANES), lanes][row:row + 1]

        def angle(j, sums):
            if isinstance(j[0], int) and (j[1] == 0 or 2 * j[1] == 3 * (waves - 1) + 1):
                return plain_angle(j, sums)
            even = [zero] * FIELDS
            odd = [zero] * FIELDS
            for k in range(slots):
                cosine = trig("cosine", k, j)
                sine = trig("sine", k, j)
                for field in range(FIELDS):
                    real, imag = coefs[k][field]
                    even[field] = even[field] + real * cosine if k else real * cosine
                    odd[field] = odd[field] + imag * sine if k else imag * sine
            (z_e, d_e, t_e), (z_o, d_o, t_o) = even, odd
            a_e = z_e + planet
            cosine = trig("own_cosine", 0, j)
            sine = trig("own_sine", 0, j)
            kinds = (
                (-(a_e * d_e + z_o * d_o), -(a_e * d_o + z_o * d_e)),
                (a_e * z_e + z_o * z_o, (a_e + z_e) * z_o),
                (0.5 * (z_e * z_e + z_o * z_o + d_e * d_e + d_o * d_o), z_e * z_o + d_e * d_o),
                (-(t_e * d_e + t_o * d_o), -(t_e * d_o + t_o * d_e)),
            )
            out = []
            for q, (in_even, in_odd) in enumerate(kinds):
                out.append(sums[2 * q] + in_even * cosine)
                out.append(sums[2 * q + 1] + in_odd * sine)
            return out

        def plain_angle(j, sums):
            even = [zero] * FIELDS
            for k in range(slots):
                cosine = trig("cosine", k, j)
                for field in range(FIELDS):
                    real = coefs[k][field][0]
                    even[field] = even[field] + real * cosine if k else real * cosine
            z, d, t = even
            a = z + planet
            cosine = trig("own_cosine", 0, j)
            kinds = (-(a * d), a * z, 0.5 * (z * z + d * d), -(t * d))
            out = list(sums)
            for q, kind in enumerate(kinds):
                out[2 * q] = sums[2 * q] + kind * cosine
            return out

        sums = [zero] * (2 * TERMS)
        if half <= SUBLANES:
            for row in range(half):
                sums = angle((0, row), sums)
        else:
            def group(g, sums):
                for row in range(SUBLANES):
                    sums = angle((g, row), sums)
                return sums

            sums = lax.fori_loop(0, angles // SUBLANES, group, sums)
        quad = aux_ref[starts["quad"]:starts["quad"] + pair, lanes]
        for q in range(TERMS):
            both = jnp.concatenate([sums[2 * q] * quad, sums[2 * q + 1] * quad], axis=0)
            back_scr[q * 2 * pair:(q + 1) * 2 * pair, here] = both.astype(jnp.bfloat16)

    for block in range(trim // LANES):
        products(block * LANES, 1)

    def lat_block(block, carry):
        products(pl.multiple_of(trim + block * LANES, LANES), waves)
        return carry

    lax.fori_loop(0, (lats - trim) // LANES, lat_block, 0)

    back = back_scr[...]
    groups = 2 * FIELDS
    place = lax.broadcasted_iota(jnp.int32, (levels * groups, groups * pair), 0)
    source = lax.broadcasted_iota(jnp.int32, (levels * groups, groups * pair), 1)
    chosen = (place % groups == source // pair) & (place // groups == source % pair)
    move = jnp.where(chosen, 1.0, 0.0).astype(jnp.bfloat16)
    copies = []
    for i in range(chunks):
        span = slice(i * chunk, (i + 1) * chunk)
        product = jnp.dot(back, table_ref[i], preferred_element_type=jnp.float32)
        if begin > 0:
            product = product + earlier_ref[:, span]
        if not last:
            partial_ref[:, span] = product
            continue
        odd = lax.broadcasted_iota(jnp.int32, (pair, chunk), 1) % 2 == 1
        laplace = aux_ref[starts["laplace"]:starts["laplace"] + 1, span]

        def both_rows(q, r):
            at = (2 * q + r) * pair
            rows = product[at:at + pair]
            south = pltpu.roll(rows, levels, 0)
            return rows + jnp.where(odd, -south, south)

        results = []
        for field in range(FIELDS):
            for r in range(2):
                if field == 0:
                    value = both_rows(0, r)
                elif field == 1:
                    at = starts["column"] + r * pair
                    column = aux_ref[at:at + pair, span]
                    column = column + below_scr[r:r + 1, span]
                    value = both_rows(1, r) + laplace * (column + both_rows(2, r))
                else:
                    value = both_rows(3, r)
                keep = aux_ref[starts["keep"] + r:starts["keep"] + r + 1, span]
                results.append(jnp.where(keep > 0.0, value, 0.0))
        stacked_rows = jnp.concatenate(results, axis=0).astype(jnp.bfloat16)
        ordered = jnp.dot(move, stacked_rows, preferred_element_type=jnp.float32)
        for level in range(levels):
            for field in range(FIELDS):
                at = (level * FIELDS + field) * 2
                out_scr[0, level, field, :, span] = ordered[at:at + 2].astype(jnp.bfloat16)
        there = (slice(None),) * 4 + (pl.ds(i * chunk, chunk),)
        copies.append(pltpu.make_async_copy(out_scr.at[there], out_ref.at[there], sems.at[i]))
        copies[-1].start()
    for copy in copies:
        copy.wait()


def gather_slots(waves, few, fourier, sent):
    if not few:
        return [[lax.all_gather(fourier, "band")]]
    return [[lax.ppermute(sent, "band", [(i, i ^ k) for i in range(waves)])] for k in range(1, waves)]


def on_device(spectra, legendre, assignment, circle_longitudes, coriolis, weights, thickness):
    levels, coeffs = spectra.shape[1], spectra.shape[4]
    lats = legendre.shape[2]
    waves = lax.axis_size("band")
    spacing = coeffs // waves
    few = waves == 4
    pair = 2 * levels
    rows = levels * FIELDS * 2
    chunk = 256 if coeffs % 256 == 0 else LANES
    chunks = coeffs // chunk
    smem = pl.BlockSpec(memory_space=pltpu.SMEM)
    vmem = pl.BlockSpec(memory_space=pltpu.VMEM)
    hbm = pl.BlockSpec(memory_space=pltpu.HBM)
    anywhere = pl.BlockSpec(memory_space=pl.ANY)
    trim = max(2 * spacing - 20, 0) // 4 // LANES * LANES if few else 0

    def pinned(x, space):
        return pltpu.with_memory_space_constraint(x, space)

    signed, total = pl.pallas_call(
        functools.partial(spectra_kernel, spacing),
        out_shape=(
            pltpu.VMEM((2 * rows, coeffs), jnp.bfloat16),
            jax.ShapeDtypeStruct((2, coeffs), jnp.float32),
        ),
        in_specs=[hbm] * 3,
        out_specs=(vmem, vmem),
        scratch_shapes=[
            pltpu.SMEM(assignment.shape, jnp.int32),
            pltpu.SMEM(thickness.shape, jnp.float32),
            pltpu.VMEM(spectra.shape, jnp.bfloat16),
            pltpu.VMEM((rows, coeffs), jnp.float32),
            pltpu.SemaphoreType.DMA((3,)),
        ],
        compiler_params=pltpu.CompilerParams(vmem_limit_bytes=8 << 20),
        name="spectra",
    )(*(pinned(x, pltpu.HBM) for x in (assignment, thickness, spectra)))
    fourier = jnp.dot(signed, legendre[0], preferred_element_type=jnp.float32).astype(jnp.bfloat16)
    gathered = gather_slots(waves, few, fourier, fourier[:, trim:])
    same = (jnp.arange(chunk)[:, None] == jnp.arange(chunk)[None, :]).astype(jnp.bfloat16)
    turned = jnp.einsum("kbh,ba->kha", legendre[0].reshape(chunks, chunk, lats), same,
                        preferred_element_type=jnp.float32).astype(jnp.bfloat16)

    deep = ("fld", "sub")
    places = lax.axis_size(deep)
    belows = [lax.all_gather(total, deep)]

    half, angles, starts, aux_rows = aux_layout(waves, levels)
    aux = pl.pallas_call(
        functools.partial(aux_kernel, waves, few, spacing),
        out_shape=jax.ShapeDtypeStruct((aux_rows, lats), jnp.float32),
        in_specs=[smem, smem, vmem, vmem, vmem, vmem, anywhere],
        out_specs=vmem,
        compiler_params=pltpu.CompilerParams(vmem_limit_bytes=(16 if few else 48) << 20),
        name="tables",
    )(assignment, thickness, circle_longitudes.reshape(1, lats), coriolis, weights, spectra, fourier)

    operands = [fourier] + sum((gathered[at] for at in arrival(len(gathered))), []) + belows + [aux, pinned(turned, pltpu.VMEM)]
    return pl.pallas_call(
        functools.partial(direct_kernel, waves, few, len(belows), 0, trim, tuple(len(g) for g in gathered), True),
        out_shape=jax.ShapeDtypeStruct(spectra.shape, jnp.bfloat16),
        in_specs=[vmem] * len(operands),
        out_specs=anywhere,
        scratch_shapes=[
            pltpu.VMEM((TERMS * 2 * pair, lats), jnp.bfloat16),
            pltpu.VMEM(spectra.shape, jnp.bfloat16),
            pltpu.VMEM(total.shape, jnp.float32),
            pltpu.SemaphoreType.DMA((chunks,)),
        ],
        compiler_params=pltpu.CompilerParams(vmem_limit_bytes=(24 if few else 56) << 20),
        name="direct",
    )(*operands)


def solution(mesh):
    in_specs = (
        P(("member", "band"), ("fld", "sub"), None, None, None),
        P("band", None, None),
        P(),
        P(),
        P(),
        P(),
        P(("fld", "sub")),
    )
    out_specs = P(("member", "band"), ("fld", "sub"), None, None, None)
    return jax.shard_map(
        on_device, mesh=mesh, in_specs=in_specs, out_specs=out_specs, check_vma=False
    )
```

```python
import functools
import math

import jax
import jax.numpy as jnp
from jax import lax
from jax.experimental import pallas as pl
from jax.experimental.pallas import tpu as pltpu
from jax.sharding import PartitionSpec as P


FIELDS = 3
TERMS = 4
LANES = 128
SUBLANES = 8
STEP = 256


def round_up(value, multiple):
    return -(-value // multiple) * multiple


def slot_position(waves, few, slot):
    return lax.axis_index("band") ^ slot if few else slot


def inverse_kernel(spacing, chunk, assign_ref, spectra_ref, legendre_ref, fourier_ref, table_ref,
                   assign_scr, spectra_scr, rows_scr, acc_scr, sems):
    coeffs = table_ref.shape[0]
    chunks = coeffs // chunk
    heads = [
        pltpu.make_async_copy(assign_ref, assign_scr, sems.at[chunks]),
        pltpu.make_async_copy(spectra_ref, spectra_scr, sems.at[chunks + 1]),
    ]
    for copy in heads:
        copy.start()
    copies = []
    for i in range(chunks):
        span = pl.ds(i * chunk, chunk)
        copies.append(pltpu.make_async_copy(legendre_ref.at[0, span], table_ref.at[span], sems.at[i]))
        copies[-1].start()
    levels = spectra_ref.shape[1]
    rows = levels * FIELDS * 2
    out_rows = 2 * rows
    place = lax.broadcasted_iota(jnp.int32, (out_rows, rows), 0)
    source = lax.broadcasted_iota(jnp.int32, (out_rows, rows), 1)
    chosen = (place // (2 * levels) == source % (2 * FIELDS)) & (place % levels == source // (2 * FIELDS))
    move = jnp.where(chosen, 1.0, 0.0).astype(jnp.bfloat16)
    for copy in heads:
        copy.wait()
    wave = spacing * assign_scr[lax.axis_index("band")]
    for level in range(levels):
        for field in range(FIELDS):
            at = (level * FIELDS + field) * 2
            rows_scr[at:at + 2, :] = spectra_scr[0, level, field].astype(jnp.float32)
    coeff = lax.broadcasted_iota(jnp.int32, (rows, coeffs), 1)
    part = lax.broadcasted_iota(jnp.int32, (rows, coeffs), 0) % 2
    keep = (coeff < coeffs - wave) & ((part == 0) | (wave > 0))
    masked = jnp.where(keep, rows_scr[...], 0.0).astype(jnp.bfloat16)
    spread = jnp.dot(move, masked, preferred_element_type=jnp.float32)
    odd = lax.broadcasted_iota(jnp.int32, (out_rows, coeffs), 1) % 2 == 1
    south = lax.broadcasted_iota(jnp.int32, (out_rows, coeffs), 0) // levels % 2 == 1
    signed = jnp.where(odd & south, -spread, spread).astype(jnp.bfloat16)
    for i in range(chunks):
        copies[i].wait()
        span = slice(i * chunk, (i + 1) * chunk)
        product = jnp.dot(signed[:, span], table_ref[span, :], preferred_element_type=jnp.float32)
        if i == 0:
            acc_scr[...] = product
        elif i < chunks - 1:
            acc_scr[...] += product
        else:
            fourier_ref[...] = (acc_scr[...] + product).astype(jnp.bfloat16)


def cos_sin(turns):
    angle = turns * (2.0 * math.pi)
    square = angle * angle
    cosine = jnp.full_like(angle, -1.0 / math.factorial(18))
    sine = jnp.full_like(angle, 1.0 / math.factorial(17))
    for n in range(8, -1, -1):
        cosine = cosine * square + (-1.0) ** n / math.factorial(2 * n)
        if n < 8:
            sine = sine * square + (-1.0) ** n / math.factorial(2 * n + 1)
    return cosine, sine * angle


def aux_layout(waves, levels):
    half = (3 * (waves - 1) + 1) // 2 + 1
    angles = round_up(half, SUBLANES)
    pair = 2 * levels
    sizes = (("cosine", waves * angles), ("sine", waves * angles), ("own_cosine", angles), ("own_sine", angles),
             ("planet", pair), ("quad", pair), ("column", 2 * pair), ("keep", 2), ("laplace", 1))
    starts, at = {}, 0
    for name, size in sizes:
        starts[name] = at
        at += size
    return half, angles, starts, round_up(at, SUBLANES)


def aux_kernel(waves, few, spacing, assign_ref, thick_ref, counts_ref, planet_ref, quad_ref, spectra_ref, after_ref,
               aux_ref, total_ref):
    del after_ref
    levels, coeffs = spectra_ref.shape[1], spectra_ref.shape[4]
    pair = 2 * levels
    half, angles, starts, _ = aux_layout(waves, levels)
    lats = aux_ref.shape[1]
    counts = counts_ref[...].astype(jnp.float32)
    most = 3 * (waves - 1) + 1

    def attempt(p, least):
        points = p * float(spacing)
        left = points - counts * jnp.floor((points + 0.5) / counts)
        return jnp.where((left == 0.0) & (least > p), p, least)

    least = jnp.full((1, lats), float(most), jnp.float32)
    if most <= 16:
        for p in range(1, most):
            least = attempt(float(p), least)
    else:
        least = lax.fori_loop(1, most, lambda p, least: attempt(p.astype(jnp.float32), least), least)
    number = jnp.broadcast_to(least, (angles, lats))
    j = lax.broadcasted_iota(jnp.int32, (angles, lats), 0).astype(jnp.float32)
    share = jnp.where(2.0 * j <= number, jnp.where((j == 0.0) | (2.0 * j == number), 1.0, 2.0), 0.0) / number

    def slot(k, carry):
        harmonic = assign_ref[slot_position(waves, few, k)]
        turn = j * harmonic.astype(jnp.float32)
        turn = turn - number * jnp.floor((turn + 0.5) / number)
        turn = jnp.where(2.0 * turn > number, turn - number, turn) / number
        cosine, sine = cos_sin(turn)
        seen = (2 * spacing * harmonic).astype(jnp.float32) < counts
        gain = jnp.where(seen, jnp.where(harmonic == 0, 1.0, 2.0), 0.0)
        at = pl.ds(pl.multiple_of(starts["cosine"] + k * angles, SUBLANES), angles)
        aux_ref[at, :] = cosine * gain
        at = pl.ds(pl.multiple_of(starts["sine"] + k * angles, SUBLANES), angles)
        aux_ref[at, :] = -sine * gain
        mine = share * jnp.where(seen, 1.0, 0.0)
        own = k == (0 if few else lax.axis_index("band"))

        @pl.when(own)
        def _():
            aux_ref[starts["own_cosine"]:starts["own_cosine"] + angles, :] = cosine * mine
            aux_ref[starts["own_sine"]:starts["own_sine"] + angles, :] = -sine * mine

        return carry

    lax.fori_loop(0, waves, slot, 0)
    north = lax.broadcasted_iota(jnp.int32, (pair, lats), 0) < levels
    for name, ref in (("planet", planet_ref), ("quad", quad_ref)):
        aux_ref[starts[name]:starts[name] + pair, :] = jnp.where(north, ref[0:1, :], ref[1:2, :])
    wave = spacing * assign_ref[lax.axis_index("band")]
    level_at = lax.broadcasted_iota(jnp.int32, (pair, coeffs), 0) % levels
    coeff = lax.broadcasted_iota(jnp.int32, (2, coeffs), 1)
    keep = (coeff < coeffs - wave) & ((lax.broadcasted_iota(jnp.int32, (2, coeffs), 0) == 0) | (wave > 0))
    columns = [jnp.zeros((pair, coeffs), jnp.float32)] * 2
    for level in range(levels):
        weighted = jnp.where(keep, spectra_ref[0, level, 2].astype(jnp.float32), 0.0) * thick_ref[level]
        for r in range(2):
            columns[r] += jnp.where(level_at <= level, weighted[r:r + 1], 0.0)
    for r in range(2):
        at = starts["column"] + r * pair
        aux_ref[at:at + pair, :] = columns[r]
        total_ref[r:r + 1, :] = columns[r][0:1]
    aux_ref[starts["keep"]:starts["keep"] + 2, :] = jnp.where(keep, 1.0, 0.0)
    degree = wave + coeff[0:1]
    truncation = coeffs - 1
    aux_ref[starts["laplace"]:starts["laplace"] + 1, :] = (
        (degree * (degree + 1)).astype(jnp.float32) / float(truncation * (truncation + 1)))


def arrival(slots):
    return (2, 0, 1) if slots == 3 else range(slots)


def direct_kernel(waves, few, trim, own_ref, *refs):
    count = waves - 1 if few else 1
    slot_refs = [None] * count
    for at, ref in zip(arrival(count), refs):
        slot_refs[at] = ref
    below_ref, aux_ref, table_ref, out_ref, back_scr, acc_scr, out_scr, below_scr, sems = refs[count:]
    below = jnp.zeros(below_ref.shape[1:], jnp.float32)
    for p in range(1, below_ref.shape[0]):
        below += jnp.where(lax.axis_index(("fld", "sub")) < p, below_ref[p], 0.0)
    below_scr[...] = below
    levels = out_scr.shape[1]
    chunks, lats, chunk = table_ref.shape
    half, angles, starts, _ = aux_layout(waves, levels)
    pair = 2 * levels
    zero = jnp.zeros((pair, LANES), jnp.float32)

    def products(lane, slots):
        lanes = pl.ds(lane, LANES)
        coefs = []
        for k in range(slots):
            fields = []
            for field in range(FIELDS):
                rows = slice(field * 2 * pair, (field + 1) * 2 * pair)
                if not few:
                    both = slot_refs[0][k, rows, lanes].astype(jnp.float32)
                elif k == 0:
                    both = own_ref[rows, lanes].astype(jnp.float32)
                else:
                    there = pl.ds(lane - trim, LANES)
                    both = slot_refs[k - 1][rows, there].astype(jnp.float32)
                fields.append((both[:pair], both[pair:]))
            coefs.append(fields)
        planet = aux_ref[starts["planet"]:starts["planet"] + pair, lanes]

        def trig(name, k, j):
            group, row = j
            at = starts[name] + k * angles + group * SUBLANES
            if isinstance(group, int):
                return aux_ref[at + row:at + row + 1, lanes]
            return aux_ref[pl.ds(pl.multiple_of(at, SUBLANES), SUBLANES), lanes][row:row + 1]

        def angle(j, sums):
            if isinstance(j[0], int) and (j[1] == 0 or 2 * j[1] == 3 * (waves - 1) + 1):
                return plain_angle(j, sums)
            even = [zero] * FIELDS
            odd = [zero] * FIELDS
            for k in range(slots):
                cosine = trig("cosine", k, j)
                sine = trig("sine", k, j)
                for field in range(FIELDS):
                    real, imag = coefs[k][field]
                    even[field] = even[field] + real * cosine if k else real * cosine
                    odd[field] = odd[field] + imag * sine if k else imag * sine
            (z_e, d_e, t_e), (z_o, d_o, t_o) = even, odd
            a_e = z_e + planet
            cosine = trig("own_cosine", 0, j)
            sine = trig("own_sine", 0, j)
            kinds = (
                (-(a_e * d_e + z_o * d_o), -(a_e * d_o + z_o * d_e)),
                (a_e * z_e + z_o * z_o, (a_e + z_e) * z_o),
                (0.5 * (z_e * z_e + z_o * z_o + d_e * d_e + d_o * d_o), z_e * z_o + d_e * d_o),
                (-(t_e * d_e + t_o * d_o), -(t_e * d_o + t_o * d_e)),
            )
            out = []
            for q, (in_even, in_odd) in enumerate(kinds):
                out.append(sums[2 * q] + in_even * cosine)
                out.append(sums[2 * q + 1] + in_odd * sine)
            return out

        def plain_angle(j, sums):
            even = [zero] * FIELDS
            for k in range(slots):
                cosine = trig("cosine", k, j)
                for field in range(FIELDS):
                    real = coefs[k][field][0]
                    even[field] = even[field] + real * cosine if k else real * cosine
            z, d, t = even
            a = z + planet
            cosine = trig("own_cosine", 0, j)
            kinds = (-(a * d), a * z, 0.5 * (z * z + d * d), -(t * d))
            out = list(sums)
            for q, kind in enumerate(kinds):
                out[2 * q] = sums[2 * q] + kind * cosine
            return out

        sums = [zero] * (2 * TERMS)
        if half <= SUBLANES:
            for row in range(half):
                sums = angle((0, row), sums)
        else:
            def group(g, sums):
                for row in range(SUBLANES):
                    sums = angle((g, row), sums)
                return sums

            sums = lax.fori_loop(0, angles // SUBLANES, group, sums)
        quad = aux_ref[starts["quad"]:starts["quad"] + pair, lanes]
        for q in range(TERMS):
            both = jnp.concatenate([sums[2 * q] * quad, sums[2 * q + 1] * quad], axis=0)
            back_scr[q * 2 * pair:(q + 1) * 2 * pair, lanes] = both.astype(jnp.bfloat16)

    def share(first, size):
        for i in range(chunks):
            span = slice(i * chunk, (i + 1) * chunk)
            product = jnp.dot(back_scr[:, first:first + size], table_ref[i, first:first + size, :],
                              preferred_element_type=jnp.float32)
            if first == 0:
                acc_scr[:, span] = product
            else:
                acc_scr[:, span] += product

    if few:
        step = STEP if lats % STEP == 0 else LANES
        for first in range(0, lats, step):
            for lane in range(first, first + step, LANES):
                products(lane, waves if lane >= trim else 1)
            share(first, step)
    else:
        def lat_block(block, carry):
            products(pl.multiple_of(block * LANES, LANES), waves)
            return carry

        lax.fori_loop(0, lats // LANES, lat_block, 0)
        share(0, lats)

    groups = 2 * FIELDS
    place = lax.broadcasted_iota(jnp.int32, (levels * groups, groups * pair), 0)
    source = lax.broadcasted_iota(jnp.int32, (levels * groups, groups * pair), 1)
    chosen = (place % groups == source // pair) & (place // groups == source % pair)
    move = jnp.where(chosen, 1.0, 0.0).astype(jnp.bfloat16)
    copies = []
    for i in range(chunks):
        span = slice(i * chunk, (i + 1) * chunk)
        odd = lax.broadcasted_iota(jnp.int32, (pair, chunk), 1) % 2 == 1
        laplace = aux_ref[starts["laplace"]:starts["laplace"] + 1, span]

        def both_rows(q, r):
            at = (2 * q + r) * pair
            rows = acc_scr[at:at + pair, span]
            south = pltpu.roll(rows, levels, 0)
            return rows + jnp.where(odd, -south, south)

        results = []
        for field in range(FIELDS):
            for r in range(2):
                if field == 0:
                    value = both_rows(0, r)
                elif field == 1:
                    at = starts["column"] + r * pair
                    column = aux_ref[at:at + pair, span] + below_scr[r:r + 1, span]
                    value = both_rows(1, r) + laplace * (column + both_rows(2, r))
                else:
                    value = both_rows(3, r)
                keep = aux_ref[starts["keep"] + r:starts["keep"] + r + 1, span]
                results.append(jnp.where(keep > 0.0, value, 0.0))
        stacked_rows = jnp.concatenate(results, axis=0).astype(jnp.bfloat16)
        ordered = jnp.dot(move, stacked_rows, preferred_element_type=jnp.float32)
        for level in range(levels):
            for field in range(FIELDS):
                at = (level * FIELDS + field) * 2
                out_scr[0, level, field, :, span] = ordered[at:at + 2].astype(jnp.bfloat16)
        there = (slice(None),) * 4 + (pl.ds(i * chunk, chunk),)
        copies.append(pltpu.make_async_copy(out_scr.at[there], out_ref.at[there], sems.at[i]))
        copies[-1].start()
    for copy in copies:
        copy.wait()


def gather_slots(waves, few, fourier, sent):
    if not few:
        return [lax.all_gather(fourier, "band")]
    return [lax.ppermute(sent, "band", [(i, i ^ k) for i in range(waves)]) for k in range(1, waves)]


def on_device(spectra, legendre, assignment, circle_longitudes, coriolis, weights, thickness):
    levels, coeffs = spectra.shape[1], spectra.shape[4]
    lats = legendre.shape[2]
    waves = lax.axis_size("band")
    spacing = coeffs // waves
    few = waves == 4
    pair = 2 * levels
    rows = levels * FIELDS * 2
    chunk = 256 if coeffs % 256 == 0 else LANES
    chunks = coeffs // chunk
    smem = pl.BlockSpec(memory_space=pltpu.SMEM)
    vmem = pl.BlockSpec(memory_space=pltpu.VMEM)
    hbm = pl.BlockSpec(memory_space=pltpu.HBM)
    anywhere = pl.BlockSpec(memory_space=pl.ANY)
    trim = max(2 * spacing - 20, 0) // 4 // LANES * LANES if few else 0

    def pinned(x, space):
        return pltpu.with_memory_space_constraint(x, space)

    fourier, table = pl.pallas_call(
        functools.partial(inverse_kernel, spacing, chunk),
        out_shape=(
            jax.ShapeDtypeStruct((2 * rows, lats), jnp.bfloat16),
            pltpu.VMEM((coeffs, lats), jnp.bfloat16),
        ),
        in_specs=[hbm] * 3,
        out_specs=(vmem, vmem),
        scratch_shapes=[
            pltpu.SMEM(assignment.shape, jnp.int32),
            pltpu.VMEM(spectra.shape, jnp.bfloat16),
            pltpu.VMEM((rows, coeffs), jnp.float32),
            pltpu.VMEM((2 * rows, lats), jnp.float32),
            pltpu.SemaphoreType.DMA((chunks + 2,)),
        ],
        compiler_params=pltpu.CompilerParams(vmem_limit_bytes=16 << 20),
        name="inverse",
    )(*(pinned(x, pltpu.HBM) for x in (assignment, spectra, legendre)))
    gathered = gather_slots(waves, few, fourier, fourier[:, trim:])
    same = (jnp.arange(chunk)[:, None] == jnp.arange(chunk)[None, :]).astype(jnp.bfloat16)
    turned = jnp.einsum("kbh,ba->kha", table.reshape(chunks, chunk, lats), same,
                        preferred_element_type=jnp.float32).astype(jnp.bfloat16)

    half, angles, starts, aux_rows = aux_layout(waves, levels)
    aux, total = pl.pallas_call(
        functools.partial(aux_kernel, waves, few, spacing),
        out_shape=(
            jax.ShapeDtypeStruct((aux_rows, lats), jnp.float32),
            jax.ShapeDtypeStruct((2, coeffs), jnp.float32),
        ),
        in_specs=[smem, smem, vmem, vmem, vmem, vmem, anywhere],
        out_specs=(vmem, vmem),
        compiler_params=pltpu.CompilerParams(vmem_limit_bytes=(16 if few else 48) << 20),
        name="tables",
    )(assignment, thickness, circle_longitudes.reshape(1, lats), coriolis, weights, spectra, fourier)

    totals = lax.all_gather(total, ("fld", "sub"))

    operands = [fourier] + [gathered[at] for at in arrival(len(gathered))] + [totals, aux, pinned(turned, pltpu.VMEM)]
    return pl.pallas_call(
        functools.partial(direct_kernel, waves, few, trim),
        out_shape=jax.ShapeDtypeStruct(spectra.shape, jnp.bfloat16),
        in_specs=[vmem] * len(operands),
        out_specs=anywhere,
        scratch_shapes=[
            pltpu.VMEM((TERMS * 2 * pair, lats), jnp.bfloat16),
            pltpu.VMEM((TERMS * 2 * pair, coeffs), jnp.float32),
            pltpu.VMEM(spectra.shape, jnp.bfloat16),
            pltpu.VMEM(total.shape, jnp.float32),
            pltpu.SemaphoreType.DMA((chunks,)),
        ],
        compiler_params=pltpu.CompilerParams(vmem_limit_bytes=(24 if few else 56) << 20),
        name="direct",
    )(*operands)


def solution(mesh):
    in_specs = (
        P(("member", "band"), ("fld", "sub"), None, None, None),
        P("band", None, None),
        P(),
        P(),
        P(),
        P(),
        P(("fld", "sub")),
    )
    out_specs = P(("member", "band"), ("fld", "sub"), None, None, None)
    return jax.shard_map(
        on_device, mesh=mesh, in_specs=in_specs, out_specs=out_specs, check_vma=False
    )
```

```python
import functools
import math

import jax
import jax.numpy as jnp
from jax import lax
from jax.experimental import pallas as pl
from jax.experimental.pallas import tpu as pltpu
from jax.sharding import PartitionSpec as P


FIELDS = 3
TERMS = 4
LANES = 128
SUBLANES = 8
STEP = 256


def round_up(value, multiple):
    return -(-value // multiple) * multiple


def slot_position(waves, few, slot):
    return lax.axis_index("band") ^ slot if few else slot


def inverse_kernel(spacing, chunk, assign_ref, spectra_ref, legendre_ref, fourier_ref, table_ref,
                   assign_scr, spectra_scr, rows_scr, acc_scr, sems):
    coeffs = table_ref.shape[0]
    chunks = coeffs // chunk
    heads = [
        pltpu.make_async_copy(assign_ref, assign_scr, sems.at[chunks]),
        pltpu.make_async_copy(spectra_ref, spectra_scr, sems.at[chunks + 1]),
    ]
    for copy in heads:
        copy.start()
    copies = []
    for i in range(chunks):
        span = pl.ds(i * chunk, chunk)
        copies.append(pltpu.make_async_copy(legendre_ref.at[0, span], table_ref.at[span], sems.at[i]))
        copies[-1].start()
    levels = spectra_ref.shape[1]
    rows = levels * FIELDS * 2
    out_rows = 2 * rows
    place = lax.broadcasted_iota(jnp.int32, (out_rows, rows), 0)
    source = lax.broadcasted_iota(jnp.int32, (out_rows, rows), 1)
    chosen = (place // (2 * levels) == source % (2 * FIELDS)) & (place % levels == source // (2 * FIELDS))
    move = jnp.where(chosen, 1.0, 0.0).astype(jnp.bfloat16)
    for copy in heads:
        copy.wait()
    wave = spacing * assign_scr[lax.axis_index("band")]
    for level in range(levels):
        for field in range(FIELDS):
            at = (level * FIELDS + field) * 2
            rows_scr[at:at + 2, :] = spectra_scr[0, level, field].astype(jnp.float32)
    coeff = lax.broadcasted_iota(jnp.int32, (rows, coeffs), 1)
    part = lax.broadcasted_iota(jnp.int32, (rows, coeffs), 0) % 2
    keep = (coeff < coeffs - wave) & ((part == 0) | (wave > 0))
    masked = jnp.where(keep, rows_scr[...], 0.0).astype(jnp.bfloat16)
    spread = jnp.dot(move, masked, preferred_element_type=jnp.float32)
    odd = lax.broadcasted_iota(jnp.int32, (out_rows, coeffs), 1) % 2 == 1
    south = lax.broadcasted_iota(jnp.int32, (out_rows, coeffs), 0) // levels % 2 == 1
    signed = jnp.where(odd & south, -spread, spread).astype(jnp.bfloat16)
    for i in range(chunks):
        copies[i].wait()
        span = slice(i * chunk, (i + 1) * chunk)
        product = jnp.dot(signed[:, span], table_ref[span, :], preferred_element_type=jnp.float32)
        if i == 0:
            acc_scr[...] = product
        elif i < chunks - 1:
            acc_scr[...] += product
        else:
            fourier_ref[...] = (acc_scr[...] + product).astype(jnp.bfloat16)


def cos_sin(turns):
    angle = turns * (2.0 * math.pi)
    square = angle * angle
    cosine = jnp.full_like(angle, -1.0 / math.factorial(18))
    sine = jnp.full_like(angle, 1.0 / math.factorial(17))
    for n in range(8, -1, -1):
        cosine = cosine * square + (-1.0) ** n / math.factorial(2 * n)
        if n < 8:
            sine = sine * square + (-1.0) ** n / math.factorial(2 * n + 1)
    return cosine, sine * angle


def aux_layout(waves, levels):
    half = (3 * (waves - 1) + 1) // 2 + 1
    angles = round_up(half, SUBLANES)
    pair = 2 * levels
    sizes = (("cosine", waves * angles), ("sine", waves * angles), ("own_cosine", angles), ("own_sine", angles),
             ("planet", pair), ("quad", pair), ("column", 2 * pair), ("keep", 2), ("laplace", 1))
    starts, at = {}, 0
    for name, size in sizes:
        starts[name] = at
        at += size
    return half, angles, starts, round_up(at, SUBLANES)


def aux_kernel(waves, few, spacing, assign_ref, thick_ref, counts_ref, planet_ref, quad_ref, spectra_ref, after_ref,
               aux_ref, total_ref):
    del after_ref
    levels, coeffs = spectra_ref.shape[1], spectra_ref.shape[4]
    pair = 2 * levels
    half, angles, starts, _ = aux_layout(waves, levels)
    lats = aux_ref.shape[1]
    counts = counts_ref[...].astype(jnp.float32)
    most = 3 * (waves - 1) + 1

    def attempt(p, least):
        points = p * float(spacing)
        left = points - counts * jnp.floor((points + 0.5) / counts)
        return jnp.where((left == 0.0) & (least > p), p, least)

    least = jnp.full((1, lats), float(most), jnp.float32)
    if most <= 16:
        for p in range(1, most):
            least = attempt(float(p), least)
    else:
        least = lax.fori_loop(1, most, lambda p, least: attempt(p.astype(jnp.float32), least), least)
    number = jnp.broadcast_to(least, (angles, lats))
    j = lax.broadcasted_iota(jnp.int32, (angles, lats), 0).astype(jnp.float32)
    share = jnp.where(2.0 * j <= number, jnp.where((j == 0.0) | (2.0 * j == number), 1.0, 2.0), 0.0) / number

    def trig(multiple):
        turn = j * multiple
        turn = turn - number * jnp.floor((turn + 0.5) / number)
        turn = jnp.where(2.0 * turn > number, turn - number, turn) / number
        return cos_sin(turn)

    if few:
        harmonics = [(jnp.ones_like(j), jnp.zeros_like(j)), trig(1.0)]
        for _ in range(2, waves):
            (cosine, sine), (once, across) = harmonics[-1], harmonics[1]
            harmonics.append((cosine * once - sine * across, sine * once + cosine * across))

    def slot(k, carry):
        harmonic = assign_ref[slot_position(waves, few, k)]
        if few:
            cosine, sine = harmonics[0]
            for a in range(1, waves):
                cosine = jnp.where(harmonic == a, harmonics[a][0], cosine)
                sine = jnp.where(harmonic == a, harmonics[a][1], sine)
        else:
            cosine, sine = trig(harmonic.astype(jnp.float32))
        seen = (2 * spacing * harmonic).astype(jnp.float32) < counts
        gain = jnp.where(seen, jnp.where(harmonic == 0, 1.0, 2.0), 0.0)
        for name, value in (("cosine", cosine * gain), ("sine", -sine * gain)):
            at = starts[name] + k * angles
            aux_ref[pl.ds(at if few else pl.multiple_of(at, SUBLANES), angles), :] = value
        mine = share * jnp.where(seen, 1.0, 0.0)

        def keep_own():
            aux_ref[starts["own_cosine"]:starts["own_cosine"] + angles, :] = cosine * mine
            aux_ref[starts["own_sine"]:starts["own_sine"] + angles, :] = -sine * mine

        if not few:
            pl.when(k == lax.axis_index("band"))(keep_own)
        elif k == 0:
            keep_own()
        return carry

    if few:
        for k in range(waves):
            slot(k, 0)
    else:
        lax.fori_loop(0, waves, slot, 0)
    north = lax.broadcasted_iota(jnp.int32, (pair, lats), 0) < levels
    for name, ref in (("planet", planet_ref), ("quad", quad_ref)):
        aux_ref[starts[name]:starts[name] + pair, :] = jnp.where(north, ref[0:1, :], ref[1:2, :])
    wave = spacing * assign_ref[lax.axis_index("band")]
    level_at = lax.broadcasted_iota(jnp.int32, (pair, coeffs), 0) % levels
    coeff = lax.broadcasted_iota(jnp.int32, (2, coeffs), 1)
    keep = (coeff < coeffs - wave) & ((lax.broadcasted_iota(jnp.int32, (2, coeffs), 0) == 0) | (wave > 0))
    columns = [jnp.zeros((pair, coeffs), jnp.float32)] * 2
    for level in range(levels):
        weighted = jnp.where(keep, spectra_ref[0, level, 2].astype(jnp.float32), 0.0) * thick_ref[level]
        for r in range(2):
            columns[r] += jnp.where(level_at <= level, weighted[r:r + 1], 0.0)
    for r in range(2):
        at = starts["column"] + r * pair
        aux_ref[at:at + pair, :] = columns[r]
        total_ref[r:r + 1, :] = columns[r][0:1]
    aux_ref[starts["keep"]:starts["keep"] + 2, :] = jnp.where(keep, 1.0, 0.0)
    degree = wave + coeff[0:1]
    truncation = coeffs - 1
    aux_ref[starts["laplace"]:starts["laplace"] + 1, :] = (
        (degree * (degree + 1)).astype(jnp.float32) / float(truncation * (truncation + 1)))


def arrival(slots):
    return (2, 0, 1) if slots == 3 else range(slots)


def direct_kernel(waves, few, trim, own_ref, *refs):
    count = waves - 1 if few else 1
    slot_refs = [None] * count
    for at, ref in zip(arrival(count), refs):
        slot_refs[at] = ref
    below_ref, aux_ref, table_ref, out_ref, back_scr, acc_scr, out_scr, below_scr, sems = refs[count:]
    below = jnp.zeros(below_ref.shape[1:], jnp.float32)
    for p in range(1, below_ref.shape[0]):
        below += jnp.where(lax.axis_index(("fld", "sub")) < p, below_ref[p], 0.0)
    below_scr[...] = below
    levels = out_scr.shape[1]
    chunks, lats, chunk = table_ref.shape
    half, angles, starts, _ = aux_layout(waves, levels)
    pair = 2 * levels
    zero = jnp.zeros((pair, LANES), jnp.float32)

    def products(lane, slots):
        lanes = pl.ds(lane, LANES)
        coefs = []
        for k in range(slots):
            fields = []
            for field in range(FIELDS):
                rows = slice(field * 2 * pair, (field + 1) * 2 * pair)
                if not few:
                    both = slot_refs[0][k, rows, lanes].astype(jnp.float32)
                elif k == 0:
                    both = own_ref[rows, lanes].astype(jnp.float32)
                else:
                    there = pl.ds(lane - trim, LANES)
                    both = slot_refs[k - 1][rows, there].astype(jnp.float32)
                fields.append((both[:pair], both[pair:]))
            coefs.append(fields)
        planet = aux_ref[starts["planet"]:starts["planet"] + pair, lanes]

        def trig(name, k, j):
            group, row = j
            at = starts[name] + k * angles + group * SUBLANES
            if isinstance(group, int):
                return aux_ref[at + row:at + row + 1, lanes]
            return aux_ref[pl.ds(pl.multiple_of(at, SUBLANES), SUBLANES), lanes][row:row + 1]

        def angle(j, sums):
            if isinstance(j[0], int) and (j[1] == 0 or 2 * j[1] == 3 * (waves - 1) + 1):
                return plain_angle(j, sums)
            even = [zero] * FIELDS
            odd = [zero] * FIELDS
            for k in range(slots):
                cosine = trig("cosine", k, j)
                sine = trig("sine", k, j)
                for field in range(FIELDS):
                    real, imag = coefs[k][field]
                    even[field] = even[field] + real * cosine if k else real * cosine
                    odd[field] = odd[field] + imag * sine if k else imag * sine
            (z_e, d_e, t_e), (z_o, d_o, t_o) = even, odd
            a_e = z_e + planet
            cosine = trig("own_cosine", 0, j)
            sine = trig("own_sine", 0, j)
            kinds = (
                (-(a_e * d_e + z_o * d_o), -(a_e * d_o + z_o * d_e)),
                (a_e * z_e + z_o * z_o, (a_e + z_e) * z_o),
                (0.5 * (z_e * z_e + z_o * z_o + d_e * d_e + d_o * d_o), z_e * z_o + d_e * d_o),
                (-(t_e * d_e + t_o * d_o), -(t_e * d_o + t_o * d_e)),
            )
            out = []
            for q, (in_even, in_odd) in enumerate(kinds):
                out.append(sums[2 * q] + in_even * cosine)
                out.append(sums[2 * q + 1] + in_odd * sine)
            return out

        def plain_angle(j, sums):
            even = [zero] * FIELDS
            for k in range(slots):
                cosine = trig("cosine", k, j)
                for field in range(FIELDS):
                    real = coefs[k][field][0]
                    even[field] = even[field] + real * cosine if k else real * cosine
            z, d, t = even
            a = z + planet
            cosine = trig("own_cosine", 0, j)
            kinds = (-(a * d), a * z, 0.5 * (z * z + d * d), -(t * d))
            out = list(sums)
            for q, kind in enumerate(kinds):
                out[2 * q] = sums[2 * q] + kind * cosine
            return out

        sums = [zero] * (2 * TERMS)
        if half <= SUBLANES:
            for row in range(half):
                sums = angle((0, row), sums)
        else:
            def group(g, sums):
                for row in range(SUBLANES):
                    sums = angle((g, row), sums)
                return sums

            sums = lax.fori_loop(0, angles // SUBLANES, group, sums)
        quad = aux_ref[starts["quad"]:starts["quad"] + pair, lanes]
        for q in range(TERMS):
            both = jnp.concatenate([sums[2 * q] * quad, sums[2 * q + 1] * quad], axis=0)
            back_scr[q * 2 * pair:(q + 1) * 2 * pair, lanes] = both.astype(jnp.bfloat16)

    def share(first, size):
        for i in range(chunks):
            span = slice(i * chunk, (i + 1) * chunk)
            product = jnp.dot(back_scr[:, first:first + size], table_ref[i, first:first + size, :],
                              preferred_element_type=jnp.float32)
            if first == 0:
                acc_scr[:, span] = product
            else:
                acc_scr[:, span] += product

    if few:
        step = STEP if lats % STEP == 0 else LANES
        for first in range(0, lats, step):
            for lane in range(first, first + step, LANES):
                products(lane, waves if lane >= trim else 1)
            share(first, step)
    else:
        def lat_block(block, carry):
            products(pl.multiple_of(block * LANES, LANES), waves)
            return carry

        lax.fori_loop(0, lats // LANES, lat_block, 0)
        share(0, lats)

    groups = 2 * FIELDS
    place = lax.broadcasted_iota(jnp.int32, (levels * groups, groups * pair), 0)
    source = lax.broadcasted_iota(jnp.int32, (levels * groups, groups * pair), 1)
    chosen = (place % groups == source // pair) & (place // groups == source % pair)
    move = jnp.where(chosen, 1.0, 0.0).astype(jnp.bfloat16)
    copies = []
    for i in range(chunks):
        span = slice(i * chunk, (i + 1) * chunk)
        odd = lax.broadcasted_iota(jnp.int32, (pair, chunk), 1) % 2 == 1
        laplace = aux_ref[starts["laplace"]:starts["laplace"] + 1, span]

        def both_rows(q, r):
            at = (2 * q + r) * pair
            rows = acc_scr[at:at + pair, span]
            south = pltpu.roll(rows, levels, 0)
            return rows + jnp.where(odd, -south, south)

        results = []
        for field in range(FIELDS):
            for r in range(2):
                if field == 0:
                    value = both_rows(0, r)
                elif field == 1:
                    at = starts["column"] + r * pair
                    column = aux_ref[at:at + pair, span] + below_scr[r:r + 1, span]
                    value = both_rows(1, r) + laplace * (column + both_rows(2, r))
                else:
                    value = both_rows(3, r)
                keep = aux_ref[starts["keep"] + r:starts["keep"] + r + 1, span]
                results.append(jnp.where(keep > 0.0, value, 0.0))
        stacked_rows = jnp.concatenate(results, axis=0).astype(jnp.bfloat16)
        ordered = jnp.dot(move, stacked_rows, preferred_element_type=jnp.float32)
        for level in range(levels):
            for field in range(FIELDS):
                at = (level * FIELDS + field) * 2
                out_scr[0, level, field, :, span] = ordered[at:at + 2].astype(jnp.bfloat16)
        there = (slice(None),) * 4 + (pl.ds(i * chunk, chunk),)
        copies.append(pltpu.make_async_copy(out_scr.at[there], out_ref.at[there], sems.at[i]))
        copies[-1].start()
    for copy in copies:
        copy.wait()


def gather_slots(waves, few, fourier, sent):
    if not few:
        return [lax.all_gather(fourier, "band")]
    return [lax.ppermute(sent, "band", [(i, i ^ k) for i in range(waves)]) for k in range(1, waves)]


def on_device(spectra, legendre, assignment, circle_longitudes, coriolis, weights, thickness):
    levels, coeffs = spectra.shape[1], spectra.shape[4]
    lats = legendre.shape[2]
    waves = lax.axis_size("band")
    spacing = coeffs // waves
    few = waves == 4
    pair = 2 * levels
    rows = levels * FIELDS * 2
    chunk = 256 if coeffs % 256 == 0 else LANES
    chunks = coeffs // chunk
    smem = pl.BlockSpec(memory_space=pltpu.SMEM)
    vmem = pl.BlockSpec(memory_space=pltpu.VMEM)
    hbm = pl.BlockSpec(memory_space=pltpu.HBM)
    anywhere = pl.BlockSpec(memory_space=pl.ANY)
    trim = max(2 * spacing - 20, 0) // 4 // LANES * LANES if few else 0

    def pinned(x, space):
        return pltpu.with_memory_space_constraint(x, space)

    fourier, table = pl.pallas_call(
        functools.partial(inverse_kernel, spacing, chunk),
        out_shape=(
            jax.ShapeDtypeStruct((2 * rows, lats), jnp.bfloat16),
            pltpu.VMEM((coeffs, lats), jnp.bfloat16),
        ),
        in_specs=[hbm] * 3,
        out_specs=(vmem, vmem),
        scratch_shapes=[
            pltpu.SMEM(assignment.shape, jnp.int32),
            pltpu.VMEM(spectra.shape, jnp.bfloat16),
            pltpu.VMEM((rows, coeffs), jnp.float32),
            pltpu.VMEM((2 * rows, lats), jnp.float32),
            pltpu.SemaphoreType.DMA((chunks + 2,)),
        ],
        compiler_params=pltpu.CompilerParams(vmem_limit_bytes=16 << 20),
        name="inverse",
    )(*(pinned(x, pltpu.HBM) for x in (assignment, spectra, legendre)))
    gathered = gather_slots(waves, few, fourier, fourier[:, trim:])
    same = (jnp.arange(chunk)[:, None] == jnp.arange(chunk)[None, :]).astype(jnp.bfloat16)
    turned = jnp.einsum("kbh,ba->kha", table.reshape(chunks, chunk, lats), same,
                        preferred_element_type=jnp.float32).astype(jnp.bfloat16)

    half, angles, starts, aux_rows = aux_layout(waves, levels)
    aux, total = pl.pallas_call(
        functools.partial(aux_kernel, waves, few, spacing),
        out_shape=(
            jax.ShapeDtypeStruct((aux_rows, lats), jnp.float32),
            jax.ShapeDtypeStruct((2, coeffs), jnp.float32),
        ),
        in_specs=[smem, smem, vmem, vmem, vmem, vmem, anywhere],
        out_specs=(vmem, vmem),
        compiler_params=pltpu.CompilerParams(vmem_limit_bytes=(16 if few else 48) << 20),
        name="tables",
    )(assignment, thickness, circle_longitudes.reshape(1, lats), coriolis, weights, spectra, fourier)

    totals = lax.all_gather(total, ("fld", "sub"))

    operands = [fourier] + [gathered[at] for at in arrival(len(gathered))] + [totals, aux, pinned(turned, pltpu.VMEM)]
    return pl.pallas_call(
        functools.partial(direct_kernel, waves, few, trim),
        out_shape=jax.ShapeDtypeStruct(spectra.shape, jnp.bfloat16),
        in_specs=[vmem] * len(operands),
        out_specs=anywhere,
        scratch_shapes=[
            pltpu.VMEM((TERMS * 2 * pair, lats), jnp.bfloat16),
            pltpu.VMEM((TERMS * 2 * pair, coeffs), jnp.float32),
            pltpu.VMEM(spectra.shape, jnp.bfloat16),
            pltpu.VMEM(total.shape, jnp.float32),
            pltpu.SemaphoreType.DMA((chunks,)),
        ],
        compiler_params=pltpu.CompilerParams(vmem_limit_bytes=(24 if few else 56) << 20),
        name="direct",
    )(*operands)


def solution(mesh):
    in_specs = (
        P(("member", "band"), ("fld", "sub"), None, None, None),
        P("band", None, None),
        P(),
        P(),
        P(),
        P(),
        P(("fld", "sub")),
    )
    out_specs = P(("member", "band"), ("fld", "sub"), None, None, None)
    return jax.shard_map(
        on_device, mesh=mesh, in_specs=in_specs, out_specs=out_specs, check_vma=False
    )
```

```python
import functools
import math

import jax
import jax.numpy as jnp
from jax import lax
from jax.experimental import pallas as pl
from jax.experimental.pallas import tpu as pltpu
from jax.sharding import PartitionSpec as P


FIELDS = 3
TERMS = 4
LANES = 128
SUBLANES = 8
STEP = 256


def round_up(value, multiple):
    return -(-value // multiple) * multiple


def slot_position(waves, few, slot):
    return lax.axis_index("band") ^ slot if few else slot


def inverse_kernel(spacing, chunk, trim, assign_ref, spectra_ref, legendre_ref, head_ref, fourier_ref, table_ref,
                   assign_scr, spectra_scr, rows_scr, acc_scr, sems):
    coeffs = table_ref.shape[0]
    chunks = coeffs // chunk
    heads = [
        pltpu.make_async_copy(assign_ref, assign_scr, sems.at[chunks + 1]),
        pltpu.make_async_copy(spectra_ref, spectra_scr, sems.at[chunks + 2]),
    ]
    for copy in heads:
        copy.start()
    cuts = list(range(0, coeffs, chunk)) + [coeffs - chunk // 2, coeffs]
    copies = []
    for i, (first, end) in enumerate(zip(cuts[:-1], cuts[1:])):
        span = pl.ds(first, end - first)
        copies.append(pltpu.make_async_copy(legendre_ref.at[0, span], table_ref.at[span], sems.at[i]))
        copies[-1].start()
    levels = spectra_ref.shape[1]
    rows = levels * FIELDS * 2
    out_rows = 2 * rows
    place = lax.broadcasted_iota(jnp.int32, (out_rows, rows), 0)
    source = lax.broadcasted_iota(jnp.int32, (out_rows, rows), 1)
    chosen = (place // (2 * levels) == source % (2 * FIELDS)) & (place % levels == source // (2 * FIELDS))
    move = jnp.where(chosen, 1.0, 0.0).astype(jnp.bfloat16)
    for copy in heads:
        copy.wait()
    wave = spacing * assign_scr[lax.axis_index("band")]
    for level in range(levels):
        for field in range(FIELDS):
            at = (level * FIELDS + field) * 2
            rows_scr[at:at + 2, :] = spectra_scr[0, level, field].astype(jnp.float32)
    coeff = lax.broadcasted_iota(jnp.int32, (rows, coeffs), 1)
    part = lax.broadcasted_iota(jnp.int32, (rows, coeffs), 0) % 2
    keep = (coeff < coeffs - wave) & ((part == 0) | (wave > 0))
    masked = jnp.where(keep, rows_scr[...], 0.0).astype(jnp.bfloat16)
    spread = jnp.dot(move, masked, preferred_element_type=jnp.float32)
    odd = lax.broadcasted_iota(jnp.int32, (out_rows, coeffs), 1) % 2 == 1
    south = lax.broadcasted_iota(jnp.int32, (out_rows, coeffs), 0) // levels % 2 == 1
    signed = jnp.where(odd & south, -spread, spread).astype(jnp.bfloat16)
    chunks = len(copies)
    for i in range(chunks):
        copies[i].wait()
        span = slice(cuts[i], cuts[i + 1])
        product = jnp.dot(signed[:, span], table_ref[span, :], preferred_element_type=jnp.float32)
        if i == 0:
            acc_scr[...] = product
        elif i < chunks - 1:
            acc_scr[...] += product
        else:
            if trim:
                head_ref[...] = (acc_scr[:, 0:trim] + product[:, 0:trim]).astype(jnp.bfloat16)
            fourier_ref[...] = (acc_scr[:, trim:] + product[:, trim:]).astype(jnp.bfloat16)


def cos_sin(turns):
    angle = turns * (2.0 * math.pi)
    square = angle * angle
    cosine = jnp.full_like(angle, -1.0 / math.factorial(18))
    sine = jnp.full_like(angle, 1.0 / math.factorial(17))
    for n in range(8, -1, -1):
        cosine = cosine * square + (-1.0) ** n / math.factorial(2 * n)
        if n < 8:
            sine = sine * square + (-1.0) ** n / math.factorial(2 * n + 1)
    return cosine, sine * angle


def aux_layout(waves, levels):
    half = (3 * (waves - 1) + 1) // 2 + 1
    angles = round_up(half, SUBLANES)
    pair = 2 * levels
    sizes = (("cosine", waves * angles), ("sine", waves * angles), ("own_cosine", angles), ("own_sine", angles),
             ("planet", pair), ("quad", pair), ("column", 2 * pair), ("keep", 2), ("laplace", 1))
    starts, at = {}, 0
    for name, size in sizes:
        starts[name] = at
        at += size
    return half, angles, starts, round_up(at, SUBLANES)


def aux_kernel(waves, few, spacing, assign_ref, thick_ref, counts_ref, planet_ref, quad_ref, spectra_ref, after_ref,
               aux_ref, total_ref):
    del after_ref
    levels, coeffs = spectra_ref.shape[1], spectra_ref.shape[4]
    pair = 2 * levels
    half, angles, starts, _ = aux_layout(waves, levels)
    lats = aux_ref.shape[1]
    counts = counts_ref[...].astype(jnp.float32)
    most = 3 * (waves - 1) + 1

    def attempt(p, least):
        points = p * float(spacing)
        left = points - counts * jnp.floor((points + 0.5) / counts)
        return jnp.where((left == 0.0) & (least > p), p, least)

    least = jnp.full((1, lats), float(most), jnp.float32)
    if most <= 16:
        for p in range(1, most):
            least = attempt(float(p), least)
    else:
        least = lax.fori_loop(1, most, lambda p, least: attempt(p.astype(jnp.float32), least), least)
    number = jnp.broadcast_to(least, (angles, lats))
    j = lax.broadcasted_iota(jnp.int32, (angles, lats), 0).astype(jnp.float32)
    share = jnp.where(2.0 * j <= number, jnp.where((j == 0.0) | (2.0 * j == number), 1.0, 2.0), 0.0) / number

    def trig(multiple):
        turn = j * multiple
        turn = turn - number * jnp.floor((turn + 0.5) / number)
        turn = jnp.where(2.0 * turn > number, turn - number, turn) / number
        return cos_sin(turn)

    if few:
        harmonics = [(jnp.ones_like(j), jnp.zeros_like(j)), trig(1.0)]
        for _ in range(2, waves):
            (cosine, sine), (once, across) = harmonics[-1], harmonics[1]
            harmonics.append((cosine * once - sine * across, sine * once + cosine * across))

    def slot(k, carry):
        harmonic = assign_ref[slot_position(waves, few, k)]
        if few:
            cosine, sine = harmonics[0]
            for a in range(1, waves):
                cosine = jnp.where(harmonic == a, harmonics[a][0], cosine)
                sine = jnp.where(harmonic == a, harmonics[a][1], sine)
        else:
            cosine, sine = trig(harmonic.astype(jnp.float32))
        seen = (2 * spacing * harmonic).astype(jnp.float32) < counts
        gain = jnp.where(seen, jnp.where(harmonic == 0, 1.0, 2.0), 0.0)
        for name, value in (("cosine", cosine * gain), ("sine", -sine * gain)):
            at = starts[name] + k * angles
            aux_ref[pl.ds(at if few else pl.multiple_of(at, SUBLANES), angles), :] = value
        mine = share * jnp.where(seen, 1.0, 0.0)

        def keep_own():
            aux_ref[starts["own_cosine"]:starts["own_cosine"] + angles, :] = cosine * mine
            aux_ref[starts["own_sine"]:starts["own_sine"] + angles, :] = -sine * mine

        if not few:
            pl.when(k == lax.axis_index("band"))(keep_own)
        elif k == 0:
            keep_own()
        return carry

    if few:
        for k in range(waves):
            slot(k, 0)
    else:
        lax.fori_loop(0, waves, slot, 0)
    north = lax.broadcasted_iota(jnp.int32, (pair, lats), 0) < levels
    for name, ref in (("planet", planet_ref), ("quad", quad_ref)):
        aux_ref[starts[name]:starts[name] + pair, :] = jnp.where(north, ref[0:1, :], ref[1:2, :])
    wave = spacing * assign_ref[lax.axis_index("band")]
    level_at = lax.broadcasted_iota(jnp.int32, (pair, coeffs), 0) % levels
    coeff = lax.broadcasted_iota(jnp.int32, (2, coeffs), 1)
    keep = (coeff < coeffs - wave) & ((lax.broadcasted_iota(jnp.int32, (2, coeffs), 0) == 0) | (wave > 0))
    columns = [jnp.zeros((pair, coeffs), jnp.float32)] * 2
    for level in range(levels):
        weighted = jnp.where(keep, spectra_ref[0, level, 2].astype(jnp.float32), 0.0) * thick_ref[level]
        for r in range(2):
            columns[r] += jnp.where(level_at <= level, weighted[r:r + 1], 0.0)
    for r in range(2):
        at = starts["column"] + r * pair
        aux_ref[at:at + pair, :] = columns[r]
        total_ref[r:r + 1, :] = columns[r][0:1]
    aux_ref[starts["keep"]:starts["keep"] + 2, :] = jnp.where(keep, 1.0, 0.0)
    degree = wave + coeff[0:1]
    truncation = coeffs - 1
    aux_ref[starts["laplace"]:starts["laplace"] + 1, :] = (
        (degree * (degree + 1)).astype(jnp.float32) / float(truncation * (truncation + 1)))


def arrival(slots):
    return (2, 0, 1) if slots == 3 else range(slots)


def direct_kernel(waves, few, trim, head_ref, own_ref, *refs):
    count = waves - 1 if few else 1
    slot_refs = [None] * count
    for at, ref in zip(arrival(count), refs):
        slot_refs[at] = ref
    below_ref, aux_ref, table_ref, out_ref, back_scr, acc_scr, out_scr, below_scr, sems = refs[count:]
    below = jnp.zeros(below_ref.shape[1:], jnp.float32)
    for p in range(1, below_ref.shape[0]):
        below += jnp.where(lax.axis_index(("fld", "sub")) < p, below_ref[p], 0.0)
    below_scr[...] = below
    levels = out_scr.shape[1]
    chunks, lats, chunk = table_ref.shape
    half, angles, starts, _ = aux_layout(waves, levels)
    pair = 2 * levels
    zero = jnp.zeros((pair, LANES), jnp.float32)

    def products(lane, slots):
        lanes = pl.ds(lane, LANES)
        coefs = []
        for k in range(slots):
            fields = []
            for field in range(FIELDS):
                rows = slice(field * 2 * pair, (field + 1) * 2 * pair)
                if not few:
                    both = slot_refs[0][k, rows, lanes].astype(jnp.float32)
                elif lane < trim:
                    both = head_ref[rows, lanes].astype(jnp.float32)
                else:
                    ref = slot_refs[k - 1] if k else own_ref
                    both = ref[rows, pl.ds(lane - trim, LANES)].astype(jnp.float32)
                fields.append((both[:pair], both[pair:]))
            coefs.append(fields)
        planet = aux_ref[starts["planet"]:starts["planet"] + pair, lanes]

        def trig(name, k, j):
            group, row = j
            at = starts[name] + k * angles + group * SUBLANES
            if isinstance(group, int):
                return aux_ref[at + row:at + row + 1, lanes]
            return aux_ref[pl.ds(pl.multiple_of(at, SUBLANES), SUBLANES), lanes][row:row + 1]

        def angle(j, sums):
            if isinstance(j[0], int) and (j[1] == 0 or 2 * j[1] == 3 * (waves - 1) + 1):
                return plain_angle(j, sums)
            even = [zero] * FIELDS
            odd = [zero] * FIELDS
            for k in range(slots):
                cosine = trig("cosine", k, j)
                sine = trig("sine", k, j)
                for field in range(FIELDS):
                    real, imag = coefs[k][field]
                    even[field] = even[field] + real * cosine if k else real * cosine
                    odd[field] = odd[field] + imag * sine if k else imag * sine
            (z_e, d_e, t_e), (z_o, d_o, t_o) = even, odd
            a_e = z_e + planet
            cosine = trig("own_cosine", 0, j)
            sine = trig("own_sine", 0, j)
            kinds = (
                (-(a_e * d_e + z_o * d_o), -(a_e * d_o + z_o * d_e)),
                (a_e * z_e + z_o * z_o, (a_e + z_e) * z_o),
                (0.5 * (z_e * z_e + z_o * z_o + d_e * d_e + d_o * d_o), z_e * z_o + d_e * d_o),
                (-(t_e * d_e + t_o * d_o), -(t_e * d_o + t_o * d_e)),
            )
            out = []
            for q, (in_even, in_odd) in enumerate(kinds):
                out.append(sums[2 * q] + in_even * cosine)
                out.append(sums[2 * q + 1] + in_odd * sine)
            return out

        def plain_angle(j, sums):
            even = [zero] * FIELDS
            for k in range(slots):
                cosine = trig("cosine", k, j)
                for field in range(FIELDS):
                    real = coefs[k][field][0]
                    even[field] = even[field] + real * cosine if k else real * cosine
            z, d, t = even
            a = z + planet
            cosine = trig("own_cosine", 0, j)
            kinds = (-(a * d), a * z, 0.5 * (z * z + d * d), -(t * d))
            out = list(sums)
            for q, kind in enumerate(kinds):
                out[2 * q] = sums[2 * q] + kind * cosine
            return out

        sums = [zero] * (2 * TERMS)
        if half <= SUBLANES:
            for row in range(half):
                sums = angle((0, row), sums)
        else:
            def group(g, sums):
                for row in range(SUBLANES):
                    sums = angle((g, row), sums)
                return sums

            sums = lax.fori_loop(0, angles // SUBLANES, group, sums)
        quad = aux_ref[starts["quad"]:starts["quad"] + pair, lanes]
        for q in range(TERMS):
            both = jnp.concatenate([sums[2 * q] * quad, sums[2 * q + 1] * quad], axis=0)
            back_scr[q * 2 * pair:(q + 1) * 2 * pair, lanes] = both.astype(jnp.bfloat16)

    def share(first, size):
        for i in range(chunks):
            span = slice(i * chunk, (i + 1) * chunk)
            product = jnp.dot(back_scr[:, first:first + size], table_ref[i, first:first + size, :],
                              preferred_element_type=jnp.float32)
            if first == 0:
                acc_scr[:, span] = product
            else:
                acc_scr[:, span] += product

    if few:
        step = STEP if lats % STEP == 0 else LANES
        for first in range(0, lats, step):
            for lane in range(first, first + step, LANES):
                products(lane, waves if lane >= trim else 1)
            share(first, step)
    else:
        def lat_block(block, carry):
            products(pl.multiple_of(block * LANES, LANES), waves)
            return carry

        lax.fori_loop(0, lats // LANES, lat_block, 0)
        share(0, lats)

    groups = 2 * FIELDS
    place = lax.broadcasted_iota(jnp.int32, (levels * groups, groups * pair), 0)
    source = lax.broadcasted_iota(jnp.int32, (levels * groups, groups * pair), 1)
    chosen = (place % groups == source // pair) & (place // groups == source % pair)
    move = jnp.where(chosen, 1.0, 0.0).astype(jnp.bfloat16)
    copies = []
    for i in range(chunks):
        span = slice(i * chunk, (i + 1) * chunk)
        odd = lax.broadcasted_iota(jnp.int32, (pair, chunk), 1) % 2 == 1
        laplace = aux_ref[starts["laplace"]:starts["laplace"] + 1, span]

        def both_rows(q, r):
            at = (2 * q + r) * pair
            rows = acc_scr[at:at + pair, span]
            south = pltpu.roll(rows, levels, 0)
            return rows + jnp.where(odd, -south, south)

        results = []
        for field in range(FIELDS):
            for r in range(2):
                if field == 0:
                    value = both_rows(0, r)
                elif field == 1:
                    at = starts["column"] + r * pair
                    column = aux_ref[at:at + pair, span] + below_scr[r:r + 1, span]
                    value = both_rows(1, r) + laplace * (column + both_rows(2, r))
                else:
                    value = both_rows(3, r)
                keep = aux_ref[starts["keep"] + r:starts["keep"] + r + 1, span]
                results.append(jnp.where(keep > 0.0, value, 0.0))
        stacked_rows = jnp.concatenate(results, axis=0).astype(jnp.bfloat16)
        ordered = jnp.dot(move, stacked_rows, preferred_element_type=jnp.float32)
        for level in range(levels):
            for field in range(FIELDS):
                at = (level * FIELDS + field) * 2
                out_scr[0, level, field, :, span] = ordered[at:at + 2].astype(jnp.bfloat16)
        there = (slice(None),) * 4 + (pl.ds(i * chunk, chunk),)
        copies.append(pltpu.make_async_copy(out_scr.at[there], out_ref.at[there], sems.at[i]))
        copies[-1].start()
    for copy in copies:
        copy.wait()


def gather_slots(waves, few, fourier, sent):
    if not few:
        return [lax.all_gather(fourier, "band")]
    return [lax.ppermute(sent, "band", [(i, i ^ k) for i in range(waves)]) for k in range(1, waves)]


def on_device(spectra, legendre, assignment, circle_longitudes, coriolis, weights, thickness):
    levels, coeffs = spectra.shape[1], spectra.shape[4]
    lats = legendre.shape[2]
    waves = lax.axis_size("band")
    spacing = coeffs // waves
    few = waves == 4
    pair = 2 * levels
    rows = levels * FIELDS * 2
    chunk = 256 if coeffs % 256 == 0 else LANES
    chunks = coeffs // chunk
    smem = pl.BlockSpec(memory_space=pltpu.SMEM)
    vmem = pl.BlockSpec(memory_space=pltpu.VMEM)
    hbm = pl.BlockSpec(memory_space=pltpu.HBM)
    anywhere = pl.BlockSpec(memory_space=pl.ANY)
    trim = max(2 * spacing - 20, 0) // 4 // LANES * LANES if few else 0

    def pinned(x, space):
        return pltpu.with_memory_space_constraint(x, space)

    head, fourier, table = pl.pallas_call(
        functools.partial(inverse_kernel, spacing, chunk, trim),
        out_shape=(
            jax.ShapeDtypeStruct((2 * rows, max(trim, LANES)), jnp.bfloat16),
            jax.ShapeDtypeStruct((2 * rows, lats - trim), jnp.bfloat16),
            pltpu.VMEM((coeffs, lats), jnp.bfloat16),
        ),
        in_specs=[hbm] * 3,
        out_specs=(vmem, vmem, vmem),
        scratch_shapes=[
            pltpu.SMEM(assignment.shape, jnp.int32),
            pltpu.VMEM(spectra.shape, jnp.bfloat16),
            pltpu.VMEM((rows, coeffs), jnp.float32),
            pltpu.VMEM((2 * rows, lats), jnp.float32),
            pltpu.SemaphoreType.DMA((chunks + 3,)),
        ],
        compiler_params=pltpu.CompilerParams(vmem_limit_bytes=16 << 20),
        name="inverse",
    )(*(pinned(x, pltpu.HBM) for x in (assignment, spectra, legendre)))
    gathered = gather_slots(waves, few, fourier, fourier)
    same = (jnp.arange(chunk)[:, None] == jnp.arange(chunk)[None, :]).astype(jnp.bfloat16)
    turned = jnp.einsum("kbh,ba->kha", table.reshape(chunks, chunk, lats), same,
                        preferred_element_type=jnp.float32).astype(jnp.bfloat16)

    half, angles, starts, aux_rows = aux_layout(waves, levels)
    aux, total = pl.pallas_call(
        functools.partial(aux_kernel, waves, few, spacing),
        out_shape=(
            jax.ShapeDtypeStruct((aux_rows, lats), jnp.float32),
            jax.ShapeDtypeStruct((2, coeffs), jnp.float32),
        ),
        in_specs=[smem, smem, vmem, vmem, vmem, vmem, anywhere],
        out_specs=(vmem, vmem),
        compiler_params=pltpu.CompilerParams(vmem_limit_bytes=(16 if few else 48) << 20),
        name="tables",
    )(assignment, thickness, circle_longitudes.reshape(1, lats), coriolis, weights, spectra, fourier)

    totals = lax.all_gather(total, ("fld", "sub"))

    operands = [head, fourier] + [gathered[at] for at in arrival(len(gathered))] + [totals, aux, pinned(turned, pltpu.VMEM)]
    return pl.pallas_call(
        functools.partial(direct_kernel, waves, few, trim),
        out_shape=jax.ShapeDtypeStruct(spectra.shape, jnp.bfloat16),
        in_specs=[vmem] * len(operands),
        out_specs=anywhere,
        scratch_shapes=[
            pltpu.VMEM((TERMS * 2 * pair, lats), jnp.bfloat16),
            pltpu.VMEM((TERMS * 2 * pair, coeffs), jnp.float32),
            pltpu.VMEM(spectra.shape, jnp.bfloat16),
            pltpu.VMEM(total.shape, jnp.float32),
            pltpu.SemaphoreType.DMA((chunks,)),
        ],
        compiler_params=pltpu.CompilerParams(vmem_limit_bytes=(24 if few else 56) << 20),
        name="direct",
    )(*operands)


def solution(mesh):
    in_specs = (
        P(("member", "band"), ("fld", "sub"), None, None, None),
        P("band", None, None),
        P(),
        P(),
        P(),
        P(),
        P(("fld", "sub")),
    )
    out_specs = P(("member", "band"), ("fld", "sub"), None, None, None)
    return jax.shard_map(
        on_device, mesh=mesh, in_specs=in_specs, out_specs=out_specs, check_vma=False
    )
```

```python
import functools
import math

import jax
import jax.numpy as jnp
from jax import lax
from jax.experimental import pallas as pl
from jax.experimental.pallas import tpu as pltpu
from jax.sharding import PartitionSpec as P


FIELDS = 3
TERMS = 4
LANES = 128
SUBLANES = 8
STEP = 256


def round_up(value, multiple):
    return -(-value // multiple) * multiple


def slot_position(waves, few, slot):
    return lax.axis_index("band") ^ slot if few else slot


def inverse_kernel(spacing, chunk, trim, assign_ref, spectra_ref, legendre_ref, head_ref, fourier_ref, table_ref,
                   assign_scr, spectra_scr, rows_scr, acc_scr, sems):
    coeffs = table_ref.shape[0]
    chunks = coeffs // chunk
    heads = [
        pltpu.make_async_copy(assign_ref, assign_scr, sems.at[chunks + 1]),
        pltpu.make_async_copy(spectra_ref, spectra_scr, sems.at[chunks + 2]),
    ]
    for copy in heads:
        copy.start()
    cuts = list(range(0, coeffs, chunk)) + [coeffs - chunk // 2, coeffs]
    copies = []
    for i, (first, end) in enumerate(zip(cuts[:-1], cuts[1:])):
        span = pl.ds(first, end - first)
        copies.append(pltpu.make_async_copy(legendre_ref.at[0, span], table_ref.at[span], sems.at[i]))
        copies[-1].start()
    levels = spectra_ref.shape[1]
    rows = levels * FIELDS * 2
    out_rows = 2 * rows
    place = lax.broadcasted_iota(jnp.int32, (out_rows, rows), 0)
    source = lax.broadcasted_iota(jnp.int32, (out_rows, rows), 1)
    chosen = (place // (2 * levels) == source % (2 * FIELDS)) & (place % levels == source // (2 * FIELDS))
    move = jnp.where(chosen, 1.0, 0.0).astype(jnp.bfloat16)
    for copy in heads:
        copy.wait()
    wave = spacing * assign_scr[lax.axis_index("band")]
    for level in range(levels):
        for field in range(FIELDS):
            at = (level * FIELDS + field) * 2
            rows_scr[at:at + 2, :] = spectra_scr[0, level, field].astype(jnp.float32)
    coeff = lax.broadcasted_iota(jnp.int32, (rows, coeffs), 1)
    part = lax.broadcasted_iota(jnp.int32, (rows, coeffs), 0) % 2
    keep = (coeff < coeffs - wave) & ((part == 0) | (wave > 0))
    masked = jnp.where(keep, rows_scr[...], 0.0).astype(jnp.bfloat16)
    spread = jnp.dot(move, masked, preferred_element_type=jnp.float32)
    odd = lax.broadcasted_iota(jnp.int32, (out_rows, coeffs), 1) % 2 == 1
    south = lax.broadcasted_iota(jnp.int32, (out_rows, coeffs), 0) // levels % 2 == 1
    signed = jnp.where(odd & south, -spread, spread).astype(jnp.bfloat16)
    chunks = len(copies)
    for i in range(chunks):
        copies[i].wait()
        span = slice(cuts[i], cuts[i + 1])
        product = jnp.dot(signed[:, span], table_ref[span, :], preferred_element_type=jnp.float32)
        if i == 0:
            acc_scr[...] = product
        elif i < chunks - 1:
            acc_scr[...] += product
        else:
            if trim:
                head_ref[...] = (acc_scr[:, 0:trim] + product[:, 0:trim]).astype(jnp.bfloat16)
            fourier_ref[...] = (acc_scr[:, trim:] + product[:, trim:]).astype(jnp.bfloat16)


def cos_sin(turns):
    angle = turns * (2.0 * math.pi)
    square = angle * angle
    cosine = jnp.full_like(angle, -1.0 / math.factorial(18))
    sine = jnp.full_like(angle, 1.0 / math.factorial(17))
    for n in range(8, -1, -1):
        cosine = cosine * square + (-1.0) ** n / math.factorial(2 * n)
        if n < 8:
            sine = sine * square + (-1.0) ** n / math.factorial(2 * n + 1)
    return cosine, sine * angle


def aux_layout(waves, levels):
    half = (3 * (waves - 1) + 1) // 2 + 1
    angles = round_up(half, SUBLANES)
    pair = 2 * levels
    sizes = (("cosine", waves * angles), ("sine", waves * angles), ("own_cosine", angles), ("own_sine", angles),
             ("planet", pair), ("quad", pair), ("column", 2 * pair), ("keep", 2), ("laplace", 1))
    starts, at = {}, 0
    for name, size in sizes:
        starts[name] = at
        at += size
    return half, angles, starts, round_up(at, SUBLANES)


def aux_kernel(waves, few, spacing, assign_ref, thick_ref, counts_ref, planet_ref, quad_ref, spectra_ref, after_ref,
               aux_ref, total_ref):
    del after_ref
    levels, coeffs = spectra_ref.shape[1], spectra_ref.shape[4]
    pair = 2 * levels
    half, angles, starts, _ = aux_layout(waves, levels)
    lats = aux_ref.shape[1]
    counts = counts_ref[...].astype(jnp.float32)
    most = 3 * (waves - 1) + 1

    def attempt(p, least):
        points = p * float(spacing)
        left = points - counts * jnp.floor((points + 0.5) / counts)
        return jnp.where((left == 0.0) & (least > p), p, least)

    least = jnp.full((1, lats), float(most), jnp.float32)
    if most <= 16:
        for p in range(1, most):
            least = attempt(float(p), least)
    else:
        least = lax.fori_loop(1, most, lambda p, least: attempt(p.astype(jnp.float32), least), least)
    number = jnp.broadcast_to(least, (angles, lats))
    j = lax.broadcasted_iota(jnp.int32, (angles, lats), 0).astype(jnp.float32)
    share = jnp.where(2.0 * j <= number, jnp.where((j == 0.0) | (2.0 * j == number), 1.0, 2.0), 0.0) / number

    def trig(multiple):
        turn = j * multiple
        turn = turn - number * jnp.floor((turn + 0.5) / number)
        turn = jnp.where(2.0 * turn > number, turn - number, turn) / number
        return cos_sin(turn)

    if few:
        harmonics = [(jnp.ones_like(j), jnp.zeros_like(j)), trig(1.0)]
        for _ in range(2, waves):
            (cosine, sine), (once, across) = harmonics[-1], harmonics[1]
            harmonics.append((cosine * once - sine * across, sine * once + cosine * across))

    def slot(k, carry):
        harmonic = assign_ref[slot_position(waves, few, k)]
        if few:
            cosine, sine = harmonics[0]
            for a in range(1, waves):
                cosine = jnp.where(harmonic == a, harmonics[a][0], cosine)
                sine = jnp.where(harmonic == a, harmonics[a][1], sine)
        else:
            cosine, sine = trig(harmonic.astype(jnp.float32))
        seen = (2 * spacing * harmonic).astype(jnp.float32) < counts
        gain = jnp.where(seen, jnp.where(harmonic == 0, 1.0, 2.0), 0.0)
        for name, value in (("cosine", cosine * gain), ("sine", -sine * gain)):
            at = starts[name] + k * angles
            aux_ref[pl.ds(at if few else pl.multiple_of(at, SUBLANES), angles), :] = value
        mine = share * jnp.where(seen, 1.0, 0.0)

        def keep_own():
            aux_ref[starts["own_cosine"]:starts["own_cosine"] + angles, :] = cosine * mine
            aux_ref[starts["own_sine"]:starts["own_sine"] + angles, :] = -sine * mine

        if not few:
            pl.when(k == lax.axis_index("band"))(keep_own)
        elif k == 0:
            keep_own()
        return carry

    if few:
        for k in range(waves):
            slot(k, 0)
    else:
        lax.fori_loop(0, waves, slot, 0)
    north = lax.broadcasted_iota(jnp.int32, (pair, lats), 0) < levels
    for name, ref in (("planet", planet_ref), ("quad", quad_ref)):
        aux_ref[starts[name]:starts[name] + pair, :] = jnp.where(north, ref[0:1, :], ref[1:2, :])
    wave = spacing * assign_ref[lax.axis_index("band")]
    level_at = lax.broadcasted_iota(jnp.int32, (pair, coeffs), 0) % levels
    coeff = lax.broadcasted_iota(jnp.int32, (2, coeffs), 1)
    keep = (coeff < coeffs - wave) & ((lax.broadcasted_iota(jnp.int32, (2, coeffs), 0) == 0) | (wave > 0))
    columns = [jnp.zeros((pair, coeffs), jnp.float32)] * 2
    for level in range(levels):
        weighted = jnp.where(keep, spectra_ref[0, level, 2].astype(jnp.float32), 0.0) * thick_ref[level]
        for r in range(2):
            columns[r] += jnp.where(level_at <= level, weighted[r:r + 1], 0.0)
    for r in range(2):
        at = starts["column"] + r * pair
        aux_ref[at:at + pair, :] = columns[r]
        total_ref[r:r + 1, :] = columns[r][0:1]
    aux_ref[starts["keep"]:starts["keep"] + 2, :] = jnp.where(keep, 1.0, 0.0)
    degree = wave + coeff[0:1]
    truncation = coeffs - 1
    aux_ref[starts["laplace"]:starts["laplace"] + 1, :] = (
        (degree * (degree + 1)).astype(jnp.float32) / float(truncation * (truncation + 1)))


def arrival(slots):
    return (2, 0, 1) if slots == 3 else range(slots)


def direct_kernel(waves, few, trim, head_ref, own_ref, *refs):
    count = waves - 1 if few else 1
    slot_refs = [None] * count
    for at, ref in zip(arrival(count), refs):
        slot_refs[at] = ref
    below_ref, aux_ref, table_ref, out_ref, back_scr, acc_scr, out_scr, below_scr, sems = refs[count:]
    below = jnp.zeros(below_ref.shape[1:], jnp.float32)
    for p in range(1, below_ref.shape[0]):
        below += jnp.where(lax.axis_index(("fld", "sub")) < p, below_ref[p], 0.0)
    below_scr[...] = below
    levels = out_scr.shape[1]
    chunks, lats, chunk = table_ref.shape
    half, angles, starts, _ = aux_layout(waves, levels)
    pair = 2 * levels
    zero = jnp.zeros((pair, LANES), jnp.float32)

    def products(lane, slots):
        lanes = pl.ds(lane, LANES)
        coefs = []
        for k in range(slots):
            fields = []
            for field in range(FIELDS):
                rows = slice(field * 2 * pair, (field + 1) * 2 * pair)
                if not few:
                    both = slot_refs[0][k, rows, lanes].astype(jnp.float32)
                elif lane < trim:
                    both = head_ref[rows, lanes].astype(jnp.float32)
                else:
                    ref = slot_refs[k - 1] if k else own_ref
                    both = ref[rows, pl.ds(lane - trim, LANES)].astype(jnp.float32)
                fields.append((both[:pair], both[pair:]))
            coefs.append(fields)
        planet = aux_ref[starts["planet"]:starts["planet"] + pair, lanes]

        def trig(name, k, j):
            group, row = j
            at = starts[name] + k * angles + group * SUBLANES
            if isinstance(group, int):
                return aux_ref[at + row:at + row + 1, lanes]
            return aux_ref[pl.ds(pl.multiple_of(at, SUBLANES), SUBLANES), lanes][row:row + 1]

        def angle(j, sums):
            if isinstance(j[0], int) and (j[1] == 0 or 2 * j[1] == 3 * (waves - 1) + 1):
                return plain_angle(j, sums)
            even = [zero] * FIELDS
            odd = [zero] * FIELDS
            for k in range(slots):
                cosine = trig("cosine", k, j)
                sine = trig("sine", k, j)
                for field in range(FIELDS):
                    real, imag = coefs[k][field]
                    even[field] = even[field] + real * cosine if k else real * cosine
                    odd[field] = odd[field] + imag * sine if k else imag * sine
            (z_e, d_e, t_e), (z_o, d_o, t_o) = even, odd
            a_e = z_e + planet
            cosine = trig("own_cosine", 0, j)
            sine = trig("own_sine", 0, j)
            kinds = (
                (-(a_e * d_e + z_o * d_o), -(a_e * d_o + z_o * d_e)),
                (a_e * z_e + z_o * z_o, (a_e + z_e) * z_o),
                (0.5 * (z_e * z_e + z_o * z_o + d_e * d_e + d_o * d_o), z_e * z_o + d_e * d_o),
                (-(t_e * d_e + t_o * d_o), -(t_e * d_o + t_o * d_e)),
            )
            out = []
            for q, (in_even, in_odd) in enumerate(kinds):
                out.append(sums[2 * q] + in_even * cosine)
                out.append(sums[2 * q + 1] + in_odd * sine)
            return out

        def plain_angle(j, sums):
            even = [zero] * FIELDS
            for k in range(slots):
                cosine = trig("cosine", k, j)
                for field in range(FIELDS):
                    real = coefs[k][field][0]
                    even[field] = even[field] + real * cosine if k else real * cosine
            z, d, t = even
            a = z + planet
            cosine = trig("own_cosine", 0, j)
            kinds = (-(a * d), a * z, 0.5 * (z * z + d * d), -(t * d))
            out = list(sums)
            for q, kind in enumerate(kinds):
                out[2 * q] = sums[2 * q] + kind * cosine
            return out

        sums = [zero] * (2 * TERMS)
        if half <= SUBLANES:
            for row in range(half):
                sums = angle((0, row), sums)
        else:
            def group(g, sums):
                for row in range(SUBLANES):
                    sums = angle((g, row), sums)
                return sums

            sums = lax.fori_loop(0, angles // SUBLANES, group, sums)
        quad = aux_ref[starts["quad"]:starts["quad"] + pair, lanes]
        for q in range(TERMS):
            both = jnp.concatenate([sums[2 * q] * quad, sums[2 * q + 1] * quad], axis=0)
            back_scr[q * 2 * pair:(q + 1) * 2 * pair, lanes] = both.astype(jnp.bfloat16)

    def share(first, size):
        for i in range(chunks):
            span = slice(i * chunk, (i + 1) * chunk)
            product = jnp.dot(back_scr[:, first:first + size], table_ref[i, first:first + size, :],
                              preferred_element_type=jnp.float32)
            if first == 0:
                acc_scr[:, span] = product
            else:
                acc_scr[:, span] += product

    if few:
        step = STEP if lats % STEP == 0 else LANES
        for first in range(0, lats, step):
            for lane in range(first, first + step, LANES):
                products(lane, waves if lane >= trim else 1)
                if first > 0 and lane == first:
                    share(first - step, step)
        share(lats - step, step)
    else:
        def lat_block(block, carry):
            products(pl.multiple_of(block * LANES, LANES), waves)
            return carry

        lax.fori_loop(0, lats // LANES, lat_block, 0)
        share(0, lats)

    groups = 2 * FIELDS
    place = lax.broadcasted_iota(jnp.int32, (levels * groups, groups * pair), 0)
    source = lax.broadcasted_iota(jnp.int32, (levels * groups, groups * pair), 1)
    chosen = (place % groups == source // pair) & (place // groups == source % pair)
    move = jnp.where(chosen, 1.0, 0.0).astype(jnp.bfloat16)
    copies = []
    for i in range(chunks):
        span = slice(i * chunk, (i + 1) * chunk)
        odd = lax.broadcasted_iota(jnp.int32, (pair, chunk), 1) % 2 == 1
        laplace = aux_ref[starts["laplace"]:starts["laplace"] + 1, span]

        def both_rows(q, r):
            at = (2 * q + r) * pair
            rows = acc_scr[at:at + pair, span]
            south = pltpu.roll(rows, levels, 0)
            return rows + jnp.where(odd, -south, south)

        results = []
        for field in range(FIELDS):
            for r in range(2):
                if field == 0:
                    value = both_rows(0, r)
                elif field == 1:
                    at = starts["column"] + r * pair
                    column = aux_ref[at:at + pair, span] + below_scr[r:r + 1, span]
                    value = both_rows(1, r) + laplace * (column + both_rows(2, r))
                else:
                    value = both_rows(3, r)
                keep = aux_ref[starts["keep"] + r:starts["keep"] + r + 1, span]
                results.append(jnp.where(keep > 0.0, value, 0.0))
        stacked_rows = jnp.concatenate(results, axis=0).astype(jnp.bfloat16)
        ordered = jnp.dot(move, stacked_rows, preferred_element_type=jnp.float32)
        for level in range(levels):
            for field in range(FIELDS):
                at = (level * FIELDS + field) * 2
                out_scr[0, level, field, :, span] = ordered[at:at + 2].astype(jnp.bfloat16)
        there = (slice(None),) * 4 + (pl.ds(i * chunk, chunk),)
        copies.append(pltpu.make_async_copy(out_scr.at[there], out_ref.at[there], sems.at[i]))
        copies[-1].start()
    for copy in copies:
        copy.wait()


def gather_slots(waves, few, fourier, sent):
    if not few:
        return [lax.all_gather(fourier, "band")]
    return [lax.ppermute(sent, "band", [(i, i ^ k) for i in range(waves)]) for k in range(1, waves)]


def on_device(spectra, legendre, assignment, circle_longitudes, coriolis, weights, thickness):
    levels, coeffs = spectra.shape[1], spectra.shape[4]
    lats = legendre.shape[2]
    waves = lax.axis_size("band")
    spacing = coeffs // waves
    few = waves == 4
    pair = 2 * levels
    rows = levels * FIELDS * 2
    chunk = 256 if coeffs % 256 == 0 else LANES
    chunks = coeffs // chunk
    smem = pl.BlockSpec(memory_space=pltpu.SMEM)
    vmem = pl.BlockSpec(memory_space=pltpu.VMEM)
    hbm = pl.BlockSpec(memory_space=pltpu.HBM)
    anywhere = pl.BlockSpec(memory_space=pl.ANY)
    trim = max(2 * spacing - 20, 0) // 4 // LANES * LANES if few else 0

    def pinned(x, space):
        return pltpu.with_memory_space_constraint(x, space)

    head, fourier, table = pl.pallas_call(
        functools.partial(inverse_kernel, spacing, chunk, trim),
        out_shape=(
            jax.ShapeDtypeStruct((2 * rows, max(trim, LANES)), jnp.bfloat16),
            jax.ShapeDtypeStruct((2 * rows, lats - trim), jnp.bfloat16),
            pltpu.VMEM((coeffs, lats), jnp.bfloat16),
        ),
        in_specs=[hbm] * 3,
        out_specs=(vmem, vmem, vmem),
        scratch_shapes=[
            pltpu.SMEM(assignment.shape, jnp.int32),
            pltpu.VMEM(spectra.shape, jnp.bfloat16),
            pltpu.VMEM((rows, coeffs), jnp.float32),
            pltpu.VMEM((2 * rows, lats), jnp.float32),
            pltpu.SemaphoreType.DMA((chunks + 3,)),
        ],
        compiler_params=pltpu.CompilerParams(vmem_limit_bytes=16 << 20),
        name="inverse",
    )(*(pinned(x, pltpu.HBM) for x in (assignment, spectra, legendre)))
    gathered = gather_slots(waves, few, fourier, fourier)
    same = (jnp.arange(chunk)[:, None] == jnp.arange(chunk)[None, :]).astype(jnp.bfloat16)
    turned = jnp.einsum("kbh,ba->kha", table.reshape(chunks, chunk, lats), same,
                        preferred_element_type=jnp.float32).astype(jnp.bfloat16)

    half, angles, starts, aux_rows = aux_layout(waves, levels)
    aux, total = pl.pallas_call(
        functools.partial(aux_kernel, waves, few, spacing),
        out_shape=(
            jax.ShapeDtypeStruct((aux_rows, lats), jnp.float32),
            jax.ShapeDtypeStruct((2, coeffs), jnp.float32),
        ),
        in_specs=[smem, smem, vmem, vmem, vmem, vmem, anywhere],
        out_specs=(vmem, vmem),
        compiler_params=pltpu.CompilerParams(vmem_limit_bytes=(16 if few else 48) << 20),
        name="tables",
    )(assignment, thickness, circle_longitudes.reshape(1, lats), coriolis, weights, spectra, fourier)

    totals = lax.all_gather(total, ("fld", "sub"))

    operands = [head, fourier] + [gathered[at] for at in arrival(len(gathered))] + [totals, aux, pinned(turned, pltpu.VMEM)]
    return pl.pallas_call(
        functools.partial(direct_kernel, waves, few, trim),
        out_shape=jax.ShapeDtypeStruct(spectra.shape, jnp.bfloat16),
        in_specs=[vmem] * len(operands),
        out_specs=anywhere,
        scratch_shapes=[
            pltpu.VMEM((TERMS * 2 * pair, lats), jnp.bfloat16),
            pltpu.VMEM((TERMS * 2 * pair, coeffs), jnp.float32),
            pltpu.VMEM(spectra.shape, jnp.bfloat16),
            pltpu.VMEM(total.shape, jnp.float32),
            pltpu.SemaphoreType.DMA((chunks,)),
        ],
        compiler_params=pltpu.CompilerParams(vmem_limit_bytes=(24 if few else 56) << 20),
        name="direct",
    )(*operands)


def solution(mesh):
    in_specs = (
        P(("member", "band"), ("fld", "sub"), None, None, None),
        P("band", None, None),
        P(),
        P(),
        P(),
        P(),
        P(("fld", "sub")),
    )
    out_specs = P(("member", "band"), ("fld", "sub"), None, None, None)
    return jax.shard_map(
        on_device, mesh=mesh, in_specs=in_specs, out_specs=out_specs, check_vma=False
    )
```

```python
import functools
import math

import jax
import jax.numpy as jnp
from jax import lax
from jax.experimental import pallas as pl
from jax.experimental.pallas import tpu as pltpu
from jax.sharding import PartitionSpec as P


FIELDS = 3
TERMS = 4
LANES = 128
SUBLANES = 8
STEP = 256


def round_up(value, multiple):
    return -(-value // multiple) * multiple


def slot_position(waves, few, slot):
    return lax.axis_index("band") ^ slot if few else slot


def inverse_kernel(spacing, chunk, trim, assign_ref, spectra_ref, legendre_ref, head_ref, fourier_ref, table_ref,
                   assign_scr, spectra_scr, rows_scr, acc_scr, sems):
    coeffs = table_ref.shape[0]
    chunks = coeffs // chunk
    heads = [
        pltpu.make_async_copy(assign_ref, assign_scr, sems.at[chunks + 1]),
        pltpu.make_async_copy(spectra_ref, spectra_scr, sems.at[chunks + 2]),
    ]
    for copy in heads:
        copy.start()
    cuts = list(range(0, coeffs, chunk)) + [coeffs - chunk // 2, coeffs]
    copies = []
    for i, (first, end) in enumerate(zip(cuts[:-1], cuts[1:])):
        span = pl.ds(first, end - first)
        copies.append(pltpu.make_async_copy(legendre_ref.at[0, span], table_ref.at[span], sems.at[i]))
        copies[-1].start()
    levels = spectra_ref.shape[1]
    rows = levels * FIELDS * 2
    out_rows = 2 * rows
    place = lax.broadcasted_iota(jnp.int32, (out_rows, rows), 0)
    source = lax.broadcasted_iota(jnp.int32, (out_rows, rows), 1)
    chosen = (place // (2 * levels) == source % (2 * FIELDS)) & (place % levels == source // (2 * FIELDS))
    move = jnp.where(chosen, 1.0, 0.0).astype(jnp.bfloat16)
    for copy in heads:
        copy.wait()
    wave = spacing * assign_scr[lax.axis_index("band")]
    for level in range(levels):
        for field in range(FIELDS):
            at = (level * FIELDS + field) * 2
            rows_scr[at:at + 2, :] = spectra_scr[0, level, field].astype(jnp.float32)
    coeff = lax.broadcasted_iota(jnp.int32, (rows, coeffs), 1)
    part = lax.broadcasted_iota(jnp.int32, (rows, coeffs), 0) % 2
    keep = (coeff < coeffs - wave) & ((part == 0) | (wave > 0))
    masked = jnp.where(keep, rows_scr[...], 0.0).astype(jnp.bfloat16)
    spread = jnp.dot(move, masked, preferred_element_type=jnp.float32)
    odd = lax.broadcasted_iota(jnp.int32, (out_rows, coeffs), 1) % 2 == 1
    south = lax.broadcasted_iota(jnp.int32, (out_rows, coeffs), 0) // levels % 2 == 1
    signed = jnp.where(odd & south, -spread, spread).astype(jnp.bfloat16)
    chunks = len(copies)
    for i in range(chunks):
        copies[i].wait()
        span = slice(cuts[i], cuts[i + 1])
        product = jnp.dot(signed[:, span], table_ref[span, :], preferred_element_type=jnp.float32)
        if i == 0:
            acc_scr[...] = product
        elif i < chunks - 1:
            acc_scr[...] += product
        else:
            if trim:
                head_ref[...] = (acc_scr[:, 0:trim] + product[:, 0:trim]).astype(jnp.bfloat16)
            fourier_ref[...] = (acc_scr[:, trim:] + product[:, trim:]).astype(jnp.bfloat16)


def cos_sin(turns):
    angle = turns * (2.0 * math.pi)
    square = angle * angle
    cosine = jnp.full_like(angle, -1.0 / math.factorial(18))
    sine = jnp.full_like(angle, 1.0 / math.factorial(17))
    for n in range(8, -1, -1):
        cosine = cosine * square + (-1.0) ** n / math.factorial(2 * n)
        if n < 8:
            sine = sine * square + (-1.0) ** n / math.factorial(2 * n + 1)
    return cosine, sine * angle


def aux_layout(waves, levels):
    half = (3 * (waves - 1) + 1) // 2 + 1
    angles = round_up(half, SUBLANES)
    pair = 2 * levels
    sizes = (("cosine", waves * angles), ("sine", waves * angles), ("own_cosine", angles), ("own_sine", angles),
             ("planet", pair), ("quad", pair), ("column", 2 * pair), ("keep", 2), ("laplace", 1))
    starts, at = {}, 0
    for name, size in sizes:
        starts[name] = at
        at += size
    return half, angles, starts, round_up(at, SUBLANES)


def aux_kernel(waves, few, spacing, assign_ref, thick_ref, counts_ref, planet_ref, quad_ref, spectra_ref, after_ref,
               aux_ref, total_ref):
    del after_ref
    levels, coeffs = spectra_ref.shape[1], spectra_ref.shape[4]
    pair = 2 * levels
    half, angles, starts, _ = aux_layout(waves, levels)
    lats = aux_ref.shape[1]
    counts = counts_ref[...].astype(jnp.float32)
    most = 3 * (waves - 1) + 1

    def attempt(p, least):
        points = p * float(spacing)
        left = points - counts * jnp.floor((points + 0.5) / counts)
        return jnp.where((left == 0.0) & (least > p), p, least)

    least = jnp.full((1, lats), float(most), jnp.float32)
    if most <= 16:
        for p in range(1, most):
            least = attempt(float(p), least)
    else:
        least = lax.fori_loop(1, most, lambda p, least: attempt(p.astype(jnp.float32), least), least)
    number = jnp.broadcast_to(least, (angles, lats))
    j = lax.broadcasted_iota(jnp.int32, (angles, lats), 0).astype(jnp.float32)
    share = jnp.where(2.0 * j <= number, jnp.where((j == 0.0) | (2.0 * j == number), 1.0, 2.0), 0.0) / number

    def trig(multiple):
        turn = j * multiple
        turn = turn - number * jnp.floor((turn + 0.5) / number)
        turn = jnp.where(2.0 * turn > number, turn - number, turn) / number
        return cos_sin(turn)

    if few:
        harmonics = [(jnp.ones_like(j), jnp.zeros_like(j)), trig(1.0)]
        for _ in range(2, waves):
            (cosine, sine), (once, across) = harmonics[-1], harmonics[1]
            harmonics.append((cosine * once - sine * across, sine * once + cosine * across))

    def slot(k, carry):
        harmonic = assign_ref[slot_position(waves, few, k)]
        if few:
            cosine, sine = harmonics[0]
            for a in range(1, waves):
                cosine = jnp.where(harmonic == a, harmonics[a][0], cosine)
                sine = jnp.where(harmonic == a, harmonics[a][1], sine)
        else:
            cosine, sine = trig(harmonic.astype(jnp.float32))
        seen = (2 * spacing * harmonic).astype(jnp.float32) < counts
        gain = jnp.where(seen, jnp.where(harmonic == 0, 1.0, 2.0), 0.0)
        for name, value in (("cosine", cosine * gain), ("sine", -sine * gain)):
            at = starts[name] + k * angles
            aux_ref[pl.ds(at if few else pl.multiple_of(at, SUBLANES), angles), :] = value
        mine = share * jnp.where(seen, 1.0, 0.0)

        def keep_own():
            aux_ref[starts["own_cosine"]:starts["own_cosine"] + angles, :] = cosine * mine
            aux_ref[starts["own_sine"]:starts["own_sine"] + angles, :] = -sine * mine

        if not few:
            pl.when(k == lax.axis_index("band"))(keep_own)
        elif k == 0:
            keep_own()
        return carry

    if few:
        for k in range(waves):
            slot(k, 0)
    else:
        lax.fori_loop(0, waves, slot, 0)
    north = lax.broadcasted_iota(jnp.int32, (pair, lats), 0) < levels
    for name, ref in (("planet", planet_ref), ("quad", quad_ref)):
        aux_ref[starts[name]:starts[name] + pair, :] = jnp.where(north, ref[0:1, :], ref[1:2, :])
    wave = spacing * assign_ref[lax.axis_index("band")]
    level_at = lax.broadcasted_iota(jnp.int32, (pair, coeffs), 0) % levels
    coeff = lax.broadcasted_iota(jnp.int32, (2, coeffs), 1)
    keep = (coeff < coeffs - wave) & ((lax.broadcasted_iota(jnp.int32, (2, coeffs), 0) == 0) | (wave > 0))
    columns = [jnp.zeros((pair, coeffs), jnp.float32)] * 2
    for level in range(levels):
        weighted = jnp.where(keep, spectra_ref[0, level, 2].astype(jnp.float32), 0.0) * thick_ref[level]
        for r in range(2):
            columns[r] += jnp.where(level_at <= level, weighted[r:r + 1], 0.0)
    for r in range(2):
        at = starts["column"] + r * pair
        aux_ref[at:at + pair, :] = columns[r]
        total_ref[r:r + 1, :] = columns[r][0:1]
    aux_ref[starts["keep"]:starts["keep"] + 2, :] = jnp.where(keep, 1.0, 0.0)
    degree = wave + coeff[0:1]
    truncation = coeffs - 1
    aux_ref[starts["laplace"]:starts["laplace"] + 1, :] = (
        (degree * (degree + 1)).astype(jnp.float32) / float(truncation * (truncation + 1)))


def arrival(slots):
    return (2, 0, 1) if slots == 3 else range(slots)


def direct_kernel(waves, few, trim, head_ref, own_ref, *refs):
    count = waves - 1 if few else 1
    slot_refs = [None] * count
    for at, ref in zip(arrival(count), refs):
        slot_refs[at] = ref
    below_ref, aux_ref, table_ref, out_ref, back_scr, acc_scr, out_scr, below_scr, sems = refs[count:]
    below = jnp.zeros(below_ref.shape[1:], jnp.float32)
    for p in range(1, below_ref.shape[0]):
        below += jnp.where(lax.axis_index(("fld", "sub")) < p, below_ref[p], 0.0)
    below_scr[...] = below
    levels = out_scr.shape[1]
    chunks, lats, chunk = table_ref.shape
    half, angles, starts, _ = aux_layout(waves, levels)
    pair = 2 * levels
    zero = jnp.zeros((pair, LANES), jnp.float32)

    def products(lane, slots):
        lanes = pl.ds(lane, LANES)
        coefs = []
        for k in range(slots):
            fields = []
            for field in range(FIELDS):
                rows = slice(field * 2 * pair, (field + 1) * 2 * pair)
                if not few:
                    both = slot_refs[0][k, rows, lanes].astype(jnp.float32)
                elif lane < trim:
                    both = head_ref[rows, lanes].astype(jnp.float32)
                else:
                    ref = slot_refs[k - 1] if k else own_ref
                    both = ref[rows, pl.ds(lane - trim, LANES)].astype(jnp.float32)
                fields.append((both[:pair], both[pair:]))
            coefs.append(fields)
        planet = aux_ref[starts["planet"]:starts["planet"] + pair, lanes]

        def trig(name, k, j):
            group, row = j
            at = starts[name] + k * angles + group * SUBLANES
            if isinstance(group, int):
                return aux_ref[at + row:at + row + 1, lanes]
            return aux_ref[pl.ds(pl.multiple_of(at, SUBLANES), SUBLANES), lanes][row:row + 1]

        def angle(j, sums):
            if isinstance(j[0], int) and (j[1] == 0 or 2 * j[1] == 3 * (waves - 1) + 1):
                return plain_angle(j, sums)
            even = [zero] * FIELDS
            odd = [zero] * FIELDS
            for k in range(slots):
                cosine = trig("cosine", k, j)
                sine = trig("sine", k, j)
                for field in range(FIELDS):
                    real, imag = coefs[k][field]
                    even[field] = even[field] + real * cosine if k else real * cosine
                    odd[field] = odd[field] + imag * sine if k else imag * sine
            (z_e, d_e, t_e), (z_o, d_o, t_o) = even, odd
            a_e = z_e + planet
            cosine = trig("own_cosine", 0, j)
            sine = trig("own_sine", 0, j)
            kinds = (
                (-(a_e * d_e + z_o * d_o), -(a_e * d_o + z_o * d_e)),
                (a_e * z_e + z_o * z_o, (a_e + z_e) * z_o),
                (0.5 * (z_e * z_e + z_o * z_o + d_e * d_e + d_o * d_o), z_e * z_o + d_e * d_o),
                (-(t_e * d_e + t_o * d_o), -(t_e * d_o + t_o * d_e)),
            )
            out = []
            for q, (in_even, in_odd) in enumerate(kinds):
                out.append(sums[2 * q] + in_even * cosine)
                out.append(sums[2 * q + 1] + in_odd * sine)
            return out

        def plain_angle(j, sums):
            even = [zero] * FIELDS
            for k in range(slots):
                cosine = trig("cosine", k, j)
                for field in range(FIELDS):
                    real = coefs[k][field][0]
                    even[field] = even[field] + real * cosine if k else real * cosine
            z, d, t = even
            a = z + planet
            cosine = trig("own_cosine", 0, j)
            kinds = (-(a * d), a * z, 0.5 * (z * z + d * d), -(t * d))
            out = list(sums)
            for q, kind in enumerate(kinds):
                out[2 * q] = sums[2 * q] + kind * cosine
            return out

        sums = [zero] * (2 * TERMS)
        if half <= SUBLANES:
            for row in range(half):
                sums = angle((0, row), sums)
        else:
            def group(g, sums):
                for row in range(SUBLANES):
                    sums = angle((g, row), sums)
                return sums

            sums = lax.fori_loop(0, angles // SUBLANES, group, sums)
        quad = aux_ref[starts["quad"]:starts["quad"] + pair, lanes]
        for q in range(TERMS):
            both = jnp.concatenate([sums[2 * q] * quad, sums[2 * q + 1] * quad], axis=0)
            back_scr[q * 2 * pair:(q + 1) * 2 * pair, lanes] = both.astype(jnp.bfloat16)

    def share(first, size):
        for i in range(chunks):
            span = slice(i * chunk, (i + 1) * chunk)
            product = jnp.dot(back_scr[:, first:first + size], table_ref[i, first:first + size, :],
                              preferred_element_type=jnp.float32)
            if first == 0:
                acc_scr[:, span] = product
            else:
                acc_scr[:, span] += product

    if few:
        step = STEP if lats % STEP == 0 else LANES
        for first in range(0, lats, step):
            for lane in range(first, first + step, LANES):
                products(lane, waves if lane >= trim else 1)
            share(first, step)
    else:
        def lat_block(block, carry):
            products(pl.multiple_of(block * LANES, LANES), waves)
            return carry

        lax.fori_loop(0, lats // LANES, lat_block, 0)
        share(0, lats)

    groups = 2 * FIELDS
    place = lax.broadcasted_iota(jnp.int32, (levels * groups, groups * pair), 0)
    source = lax.broadcasted_iota(jnp.int32, (levels * groups, groups * pair), 1)
    chosen = (place % groups == source // pair) & (place // groups == source % pair)
    move = jnp.where(chosen, 1.0, 0.0).astype(jnp.bfloat16)
    copies = []
    for i in range(chunks):
        span = slice(i * chunk, (i + 1) * chunk)
        odd = lax.broadcasted_iota(jnp.int32, (pair, chunk), 1) % 2 == 1
        laplace = aux_ref[starts["laplace"]:starts["laplace"] + 1, span]

        def both_rows(q, r):
            at = (2 * q + r) * pair
            rows = acc_scr[at:at + pair, span]
            south = pltpu.roll(rows, levels, 0)
            return rows + jnp.where(odd, -south, south)

        results = []
        for field in range(FIELDS):
            for r in range(2):
                if field == 0:
                    value = both_rows(0, r)
                elif field == 1:
                    at = starts["column"] + r * pair
                    column = aux_ref[at:at + pair, span] + below_scr[r:r + 1, span]
                    value = both_rows(1, r) + laplace * (column + both_rows(2, r))
                else:
                    value = both_rows(3, r)
                keep = aux_ref[starts["keep"] + r:starts["keep"] + r + 1, span]
                results.append(jnp.where(keep > 0.0, value, 0.0))
        stacked_rows = jnp.concatenate(results, axis=0).astype(jnp.bfloat16)
        ordered = jnp.dot(move, stacked_rows, preferred_element_type=jnp.float32)
        for level in range(levels):
            for field in range(FIELDS):
                at = (level * FIELDS + field) * 2
                out_scr[0, level, field, :, span] = ordered[at:at + 2].astype(jnp.bfloat16)
        there = (slice(None),) * 4 + (pl.ds(i * chunk, chunk),)
        copies.append(pltpu.make_async_copy(out_scr.at[there], out_ref.at[there], sems.at[i]))
        copies[-1].start()
    for copy in copies:
        copy.wait()


def gather_slots(waves, few, fourier, sent):
    if not few:
        return [lax.all_gather(fourier, "band")]
    return [lax.ppermute(sent, "band", [(i, i ^ k) for i in range(waves)]) for k in range(1, waves)]


def on_device(spectra, legendre, assignment, circle_longitudes, coriolis, weights, thickness):
    levels, coeffs = spectra.shape[1], spectra.shape[4]
    lats = legendre.shape[2]
    waves = lax.axis_size("band")
    spacing = coeffs // waves
    few = waves == 4
    pair = 2 * levels
    rows = levels * FIELDS * 2
    chunk = 256 if coeffs % 256 == 0 else LANES
    chunks = coeffs // chunk
    smem = pl.BlockSpec(memory_space=pltpu.SMEM)
    vmem = pl.BlockSpec(memory_space=pltpu.VMEM)
    hbm = pl.BlockSpec(memory_space=pltpu.HBM)
    anywhere = pl.BlockSpec(memory_space=pl.ANY)
    trim = max(2 * spacing - 20, 0) // 4 // LANES * LANES if few else 0

    def pinned(x, space):
        return pltpu.with_memory_space_constraint(x, space)

    head, fourier, table = pl.pallas_call(
        functools.partial(inverse_kernel, spacing, chunk, trim),
        out_shape=(
            jax.ShapeDtypeStruct((2 * rows, max(trim, LANES)), jnp.bfloat16),
            jax.ShapeDtypeStruct((2 * rows, lats - trim), jnp.bfloat16),
            pltpu.VMEM((coeffs, lats), jnp.bfloat16),
        ),
        in_specs=[hbm] * 3,
        out_specs=(vmem, vmem, vmem),
        scratch_shapes=[
            pltpu.SMEM(assignment.shape, jnp.int32),
            pltpu.VMEM(spectra.shape, jnp.bfloat16),
            pltpu.VMEM((rows, coeffs), jnp.float32),
            pltpu.VMEM((2 * rows, lats), jnp.float32),
            pltpu.SemaphoreType.DMA((chunks + 3,)),
        ],
        compiler_params=pltpu.CompilerParams(vmem_limit_bytes=8 << 20),
        name="inverse",
    )(*(pinned(x, pltpu.HBM) for x in (assignment, spectra, legendre)))
    gathered = gather_slots(waves, few, fourier, fourier)
    same = (jnp.arange(chunk)[:, None] == jnp.arange(chunk)[None, :]).astype(jnp.bfloat16)
    turned = jnp.einsum("kbh,ba->kha", table.reshape(chunks, chunk, lats), same,
                        preferred_element_type=jnp.float32).astype(jnp.bfloat16)

    half, angles, starts, aux_rows = aux_layout(waves, levels)
    aux, total = pl.pallas_call(
        functools.partial(aux_kernel, waves, few, spacing),
        out_shape=(
            jax.ShapeDtypeStruct((aux_rows, lats), jnp.float32),
            jax.ShapeDtypeStruct((2, coeffs), jnp.float32),
        ),
        in_specs=[smem, smem, vmem, vmem, vmem, vmem, anywhere],
        out_specs=(vmem, vmem),
        compiler_params=pltpu.CompilerParams(vmem_limit_bytes=(8 if few else 48) << 20),
        name="tables",
    )(assignment, thickness, circle_longitudes.reshape(1, lats), coriolis, weights, spectra, fourier)

    totals = lax.all_gather(total, ("fld", "sub"))

    operands = [head, fourier] + [gathered[at] for at in arrival(len(gathered))] + [totals, aux, pinned(turned, pltpu.VMEM)]
    return pl.pallas_call(
        functools.partial(direct_kernel, waves, few, trim),
        out_shape=jax.ShapeDtypeStruct(spectra.shape, jnp.bfloat16),
        in_specs=[vmem] * len(operands),
        out_specs=anywhere,
        scratch_shapes=[
            pltpu.VMEM((TERMS * 2 * pair, lats), jnp.bfloat16),
            pltpu.VMEM((TERMS * 2 * pair, coeffs), jnp.float32),
            pltpu.VMEM(spectra.shape, jnp.bfloat16),
            pltpu.VMEM(total.shape, jnp.float32),
            pltpu.SemaphoreType.DMA((chunks,)),
        ],
        compiler_params=pltpu.CompilerParams(vmem_limit_bytes=(8 if few else 56) << 20),
        name="direct",
    )(*operands)


def solution(mesh):
    in_specs = (
        P(("member", "band"), ("fld", "sub"), None, None, None),
        P("band", None, None),
        P(),
        P(),
        P(),
        P(),
        P(("fld", "sub")),
    )
    out_specs = P(("member", "band"), ("fld", "sub"), None, None, None)
    return jax.shard_map(
        on_device, mesh=mesh, in_specs=in_specs, out_specs=out_specs, check_vma=False
    )
```
